32 devices in a mesh: dp: 4 (over z), fsdp: 4 (over y, core), enc: 2 (over x).
Axes of the slice: x: 2, y: 2, z: 4, core: 2. Of those that a mesh axis runs over, the one named last changes fastest.
Arguments:
- queries: bfloat16 [3072, 4096], P(('dp', 'fsdp'), 'enc'), may hold values from -9 to 9
- nbr_keys: bfloat16 [96, 128, 4096], P('dp', 'fsdp', 'enc'), may hold values from -6 to 6
- nbr_values: bfloat16 [96, 128, 4096], P('dp', 'fsdp', 'enc'), may hold values from -6 to 6
- out_proj: bfloat16 [4096, 8192], P('enc', 'fsdp'), may hold values from -0.09375 to 0.09375
- nbr_source: int32 [48, 2], replicated, may hold values from 0 to 3, as said below
- nbr_index: int32 [48, 2], replicated, may hold values from 0 to 23
- nbr_count: int32 [48], replicated, may hold values from 1 to 2
- cotangent: bfloat16 [3072, 8192], P('dp', 'fsdp'), may hold values from -2.390625 to 2.390625
Outputs:
- attended: bfloat16 [3072, 4096], P(('dp', 'fsdp'), 'enc')
- grad_queries: bfloat16 [3072, 4096], P(('dp', 'fsdp'), 'enc')
- grad_keys: bfloat16 [96, 128, 4096], P('dp', 'fsdp', 'enc')
- grad_values: bfloat16 [96, 128, 4096], P('dp', 'fsdp', 'enc')
- grad_proj: bfloat16 [4096, 8192], P('enc', 'fsdp')
The draws below stay inside these ranges and needn't reach their ends.
Inputs may be any that keep to these rules, and one draw needn't show every extreme that they name: `nbr_source`: among the 6 slots of the spans of one device, no source group is named more than 2 times, and some group exactly 2 times.
All inputs are finite; a program needn't handle non-finite values.
Results may differ from the reference program's by a relative error of at most 0.013.
Values may be sent and summed in bfloat16 or wider, within the bound.
No kernel may reach another device: no remote copies, remote signals or barrier semaphores. Data moves between devices by JAX's collectives and lax.ppermute only.
A program may use at most 128 MiB of HBM per device.

```python
import math
import jax
import jax.numpy as jnp
from jax import lax

D = 8192
HEADS = 32
HEAD_DIM = 128
SPAN = 64
NBR_LEN = 128
SLOTS = 2
TOK_DEV = 192
HD = 4096
SPANS_DEV = 3
TOKENS = 3072
SPANS = 48
NB_GROUP = 24
NBRS = 96
N_DP = 4
N_FSDP = 4


def draw_queries(key, part):
    base = jnp.clip(jax.random.normal(jax.random.fold_in(key, 11), (TOKENS, HD), jnp.float32), -6.0, 6.0)
    return base.astype(jnp.bfloat16)


def draw_nbr_keys(key, part):
    base = jnp.clip(jax.random.normal(jax.random.fold_in(key, 21), (NBRS, NBR_LEN, HD), jnp.float32), -6.0, 6.0)
    return base.astype(jnp.bfloat16)


def draw_nbr_source(key, part):
    groups = SPANS // SPANS_DEV
    group_keys = jax.random.split(jax.random.fold_in(key, 31), groups)
    orders = jax.vmap(lambda single: jax.random.permutation(single, N_DP))(group_keys)
    positions = jnp.arange(SLOTS * SPANS_DEV) % N_DP
    return orders[:, positions].reshape(SPANS, SLOTS).astype(jnp.int32)


def draw_nbr_count(key, part):
    document_texts = SPANS // 4 + 1
    levels = jax.random.randint(jax.random.fold_in(key, 41), (document_texts,), 0, 9)
    levels = levels.at[0].set(8).at[1].set(0)
    owner = jnp.arange(SPANS) // 4
    rolls = jax.random.randint(jax.random.fold_in(key, 42), (SPANS,), 0, 8)
    return (1 + (rolls < levels[owner]).astype(jnp.int32)).astype(jnp.int32)


def set_ends(entries, own_key, smallest, top_value):
    extent = entries.shape
    index_at = [jax.random.randint(jax.random.fold_in(own_key, axis), (), 0, extent[axis]) for axis in range(len(extent))]
    entries = entries.at[tuple(index_at)].set(smallest)
    longest = extent.index(max(extent))
    index_at[longest] = (index_at[longest] + 1) % extent[longest]
    return entries.at[tuple(index_at)].set(top_value)


def block_levels(own_key, shape, cuts, smallest, high):
    loudness, own = 1.0, jax.random.fold_in(own_key, 6)
    for dim, parts in cuts:
        heights = jnp.exp(jax.random.uniform(jax.random.fold_in(own, dim), (parts,), jnp.float32, smallest / len(cuts), high / len(cuts)))
        loudness = loudness * jnp.repeat(heights, shape[dim] // parts).reshape([-1 if axis == dim else 1 for axis in range(len(shape))])
    return loudness


def bell_draw(stream_key, dims, width, reach, cuts=(), held_as=jnp.bfloat16):
    result = jax.random.normal(stream_key, dims, jnp.float32) * width
    if len(cuts) > 0:
        result = block_levels(stream_key, dims, cuts, -0.22, 0.18) * result
    return jnp.clip(result, min=-reach, max=reach).astype(held_as)


def setup_inputs(seed: int = 0) -> dict:
    splits = jax.random.split(jax.random.key(seed), 9)
    queries = draw_queries(jax.random.fold_in(splits[8], 71), 0)
    nbr_keys = draw_nbr_keys(jax.random.fold_in(splits[8], 71), 0)
    nbr_values = bell_draw(splits[2], (NBRS, NBR_LEN, HD), 1.0, 6.0, ((0, 4), (1, 4), (2, 2)))
    out_proj = bell_draw(splits[3], (HD, D), HD ** -0.5, 0.09375, ((0, 2), (1, 4)))
    nbr_source = draw_nbr_source(jax.random.fold_in(splits[8], 71), 0)
    nbr_index = set_ends(jax.random.randint(splits[5], (SPANS, SLOTS), 0, NB_GROUP), jax.random.fold_in(splits[5], 1), 0, NB_GROUP - 1).astype(jnp.int32)
    nbr_count = draw_nbr_count(jax.random.fold_in(splits[8], 71), 0)
    cotangent = bell_draw(splits[7], (TOKENS, D), 0.3, 2.390625, ((0, 4), (1, 4)))
    return {"queries": queries, "nbr_keys": nbr_keys, "nbr_values": nbr_values, "out_proj": out_proj, "nbr_source": nbr_source, "nbr_index": nbr_index, "nbr_count": nbr_count, "cotangent": cotangent}


def reference(queries, nbr_keys, nbr_values, out_proj, nbr_source, nbr_index, nbr_count, cotangent):
    scale = 1.0 / math.sqrt(HEAD_DIM)
    ident = (nbr_source * NB_GROUP + nbr_index).astype(jnp.int32)
    upstream = jnp.dot(cotangent, out_proj.T, preferred_element_type=jnp.float32).astype(jnp.bfloat16)
    live_keys = jnp.repeat(jnp.arange(SLOTS)[None, :] < nbr_count[:, None], NBR_LEN, axis=1)

    def per_span(position):
        chosen = ident[position]
        keys_here = jnp.take(nbr_keys, chosen, axis=0).reshape(SLOTS * NBR_LEN, HEADS, HEAD_DIM).astype(jnp.float32)
        values_here = jnp.take(nbr_values, chosen, axis=0).reshape(SLOTS * NBR_LEN, HEADS, HEAD_DIM).astype(jnp.float32)
        first_row = (position * SPAN).astype(jnp.int32)
        query_here = lax.dynamic_slice_in_dim(queries, first_row, SPAN, 0).reshape(SPAN, HEADS, HEAD_DIM).astype(jnp.float32)
        grad_here = lax.dynamic_slice_in_dim(upstream, first_row, SPAN, 0).reshape(SPAN, HEADS, HEAD_DIM).astype(jnp.float32)
        scores = jnp.einsum('qhd,khd->hqk', query_here, keys_here) * scale
        scores = jnp.where(live_keys[position][None, None, :], scores, -1e+30)
        peak = lax.optimization_barrier(jnp.max(scores, axis=-1, keepdims=True))
        expo = jnp.exp(scores - peak)
        probs = expo / lax.optimization_barrier(jnp.sum(expo, axis=-1, keepdims=True))
        probs_b = probs.astype(jnp.bfloat16)
        attended_here = jnp.einsum('hqk,khd->qhd', probs_b.astype(jnp.float32), values_here).astype(jnp.bfloat16)
        probability_gradient = jnp.einsum('qhd,khd->hqk', grad_here, values_here)
        centre = lax.optimization_barrier(jnp.sum(probs * probability_gradient, axis=-1, keepdims=True))
        dscores = (probs * (probability_gradient - centre) * scale).astype(jnp.bfloat16)
        grad_query = jnp.einsum('hqk,khd->qhd', dscores.astype(jnp.float32), keys_here).astype(jnp.bfloat16)
        slot_key = jnp.einsum('hqk,qhd->khd', dscores.astype(jnp.float32), query_here).astype(jnp.bfloat16)
        slot_value = jnp.einsum('hqk,qhd->khd', probs_b.astype(jnp.float32), grad_here).astype(jnp.bfloat16)
        return (attended_here, grad_query, slot_key, slot_value)
    attended, grad_queries, slot_keys, slot_values = lax.map(per_span, jnp.arange(SPANS, dtype=jnp.int32))
    attended = attended.reshape(TOKENS, HD)
    grad_queries = grad_queries.reshape(TOKENS, HD)
    flat_ident = ident.reshape(-1)
    grad_keys = jax.ops.segment_sum(slot_keys.astype(jnp.float32).reshape(SPANS * SLOTS, NBR_LEN, HD), flat_ident, num_segments=NBRS).astype(jnp.bfloat16)
    grad_values = jax.ops.segment_sum(slot_values.astype(jnp.float32).reshape(SPANS * SLOTS, NBR_LEN, HD), flat_ident, num_segments=NBRS).astype(jnp.bfloat16)
    bin_rows = TOK_DEV * N_FSDP

    def add_bin(running, position):
        first_row = (position * bin_rows).astype(jnp.int32)
        rows_att = lax.dynamic_slice_in_dim(attended, first_row, bin_rows, 0)
        rows_cot = lax.dynamic_slice_in_dim(cotangent, first_row, bin_rows, 0)
        term = jnp.dot(rows_att.T, rows_cot, preferred_element_type=jnp.float32).astype(jnp.bfloat16)
        term = lax.optimization_barrier(term)
        return (running + term.astype(jnp.float32), None)
    total, _ = lax.scan(add_bin, jnp.zeros((HD, D), jnp.float32), jnp.arange(N_DP, dtype=jnp.int32))
    grad_proj = total.astype(jnp.bfloat16)
    return (attended, grad_queries, grad_keys, grad_values, grad_proj)
```

```python
import functools
import math

import jax
import jax.numpy as jnp
from jax import lax
from jax.experimental import pallas as pl
from jax.experimental.pallas import tpu as pltpu
from jax.sharding import PartitionSpec as P

HEAD_DIM = 128
SPAN = 64
SLOTS = 2
LANES = 128
LOW = -1e30
BF16 = jnp.bfloat16
F32 = jnp.float32


def dot(a, b, dims):
    return lax.dot_general(a, b, ((dims[0], dims[1]), ((), ())), preferred_element_type=F32)


def neighbour_head(ref, n, cols):
    return jnp.concatenate([ref[p, n, :, cols] for p in range(ref.shape[0])], axis=0)


def stats_kernel(heads, scale, nbr_ref, live_ref, q_ref, up_ref, k_ref, v_ref, out_ref):
    count = q_ref.shape[0]
    base = pl.program_id(0) * count
    lane = lax.broadcasted_iota(jnp.int32, (SPAN, LANES), 1)

    def slot(r, carry):
        n = nbr_ref[base + r]
        live = live_ref[base + r] != 0

        @pl.when(live)
        def _():
            first = jnp.zeros((SPAN, LANES), F32)
            second = jnp.zeros((SPAN, LANES), F32)
            for h in range(heads):
                cols = slice(h * HEAD_DIM, (h + 1) * HEAD_DIM)
                scores = dot(q_ref[r, :, cols], neighbour_head(k_ref, n, cols), ((1,), (1,))) * scale
                dprobs = dot(up_ref[r, :, cols], neighbour_head(v_ref, n, cols), ((1,), (1,)))
                peak = jnp.max(scores, axis=1, keepdims=True)
                expo = jnp.exp(scores - peak)
                total = jnp.sum(expo, axis=1, keepdims=True)
                weighted = jnp.sum(expo * dprobs, axis=1, keepdims=True)
                first = jnp.where(lane == h, peak, first)
                first = jnp.where(lane == heads + h, weighted, first)
                second = jnp.where(lane == h, total, second)
            both = jnp.concatenate([first, second], axis=0)
            out_ref[r] = both.T[:8, :]

        @pl.when(jnp.logical_not(live))
        def _():
            out_ref[r] = jnp.zeros((8, LANES), F32)

        return carry

    lax.fori_loop(0, count, slot, 0)


def grads_kernel(heads, scale, nbr_ref, live_ref, where_ref, on_ref, stats_ref, q_ref, up_ref, k_ref, v_ref,
                 o_ref, gq_ref, gk_ref, gv_ref, acc_k, acc_v):
    count = q_ref.shape[0]
    step = pl.program_id(0)
    base = step * count
    pieces, _, piece_rows, _ = k_ref.shape

    @pl.when(step == 0)
    def _():
        acc_k[...] = jnp.zeros_like(acc_k)
        acc_v[...] = jnp.zeros_like(acc_v)

    def slot(r, carry):
        n = nbr_ref[base + r]
        live = live_ref[base + r] != 0

        @pl.when(live)
        def _():
            peaks, totals, weights = [], [], []
            for s in range(SLOTS):
                at = (base + r) * SLOTS + s
                tile = stats_ref[where_ref[at]]
                on = on_ref[at] != 0
                peaks.append(jnp.where(on, tile[:heads, :SPAN], LOW))
                totals.append(jnp.where(on, tile[:heads, SPAN:], 0.0))
                weights.append(jnp.where(on, tile[heads : 2 * heads, :SPAN], 0.0))
            peak = functools.reduce(jnp.maximum, peaks)
            factors = [jnp.exp(p - peak) for p in peaks]
            total = sum(f * t for f, t in zip(factors, totals))
            weighted = sum(f * w for f, w in zip(factors, weights))
            joined = jnp.concatenate([peak + jnp.log(total), weighted / total], axis=1)
            columns = jnp.concatenate([joined, jnp.zeros((LANES - heads, LANES), F32)], axis=0).T
            for h in range(heads):
                cols = slice(h * HEAD_DIM, (h + 1) * HEAD_DIM)
                q, up = q_ref[r, :, cols], up_ref[r, :, cols]
                keys, values = neighbour_head(k_ref, n, cols), neighbour_head(v_ref, n, cols)
                scores = dot(q, keys, ((1,), (1,))) * scale
                dprobs = dot(up, values, ((1,), (1,)))
                probs = jnp.exp(scores - columns[:SPAN, h : h + 1])
                probs_b = probs.astype(BF16)
                dscores = (probs * (dprobs - columns[SPAN:, h : h + 1]) * scale).astype(BF16)
                o_ref[r, :, cols] = dot(probs_b, values, ((1,), (0,))).astype(BF16)
                gq_ref[r, :, cols] = dot(dscores, keys, ((1,), (0,))).astype(BF16)
                acc_k[n, :, cols] += dot(dscores, q, ((0,), (0,)))
                acc_v[n, :, cols] += dot(probs_b, up, ((0,), (0,)))

        @pl.when(jnp.logical_not(live))
        def _():
            o_ref[r] = jnp.zeros(o_ref.shape[1:], BF16)
            gq_ref[r] = jnp.zeros(gq_ref.shape[1:], BF16)

        return carry

    lax.fori_loop(0, count, slot, 0)

    @pl.when(step == pl.num_programs(0) - 1)
    def _():
        def neighbour(n, carry):
            for p in range(pieces):
                rows = slice(p * piece_rows, (p + 1) * piece_rows)
                gk_ref[p, n] = acc_k[n, rows, :].astype(BF16)
                gv_ref[p, n] = acc_v[n, rows, :].astype(BF16)
            return carry

        lax.fori_loop(0, acc_k.shape[0], neighbour, 0)


def line_gather(x, axis):
    n = lax.axis_size(axis)
    rise = [(i, i + 1) for i in range(n - 1)]
    fall = [(i + 1, i) for i in range(n - 1)]
    ups, downs = [x], [x]
    for _ in range(n - 1):
        ups.append(lax.ppermute(ups[-1], axis, rise))
        downs.append(lax.ppermute(downs[-1], axis, fall))
    return [x] + [ups[r] + downs[n - r] for r in range(1, n)]


def swap(x, axis, bits):
    return lax.ppermute(x, axis, [(i, i ^ bits) for i in range(lax.axis_size(axis))])


def local(queries, nbr_keys, nbr_values, out_proj, nbr_source, nbr_index, nbr_count, cotangent):
    n_dp, n_f, n_e = lax.axis_size("dp"), lax.axis_size("fsdp"), lax.axis_size("enc")
    token_rows, width = queries.shape
    hw = width // n_f
    heads = hw // HEAD_DIM
    spans_here = token_rows // SPAN
    spans = spans_here * n_f
    slots = spans * SLOTS
    cap = (spans_here * SLOTS + n_dp - 1) // n_dp * n_f
    group, piece_rows, _ = nbr_keys.shape
    nbr_len = piece_rows * n_f
    bin_rows = token_rows * n_f
    homes = n_dp * cap
    scale = 1.0 / math.sqrt(HEAD_DIM)
    mine = lax.axis_index("dp")
    place = lax.axis_index("fsdp")
    enc = lax.axis_index("enc")

    src = nbr_source.reshape(n_dp, slots)
    idx = nbr_index.reshape(n_dp, slots)
    live = (jnp.arange(SLOTS, dtype=jnp.int32)[None, :] < nbr_count[:, None]).reshape(n_dp, slots)
    iota = jnp.arange(slots, dtype=jnp.int32)
    same = src[:, :, None] == src[:, None, :]
    rank = jnp.sum(jnp.logical_and(same, iota[None, None, :] < iota[None, :, None]), axis=2, dtype=jnp.int32)
    spot = src * cap + rank
    hit = spot[:, None, :] == jnp.arange(homes, dtype=jnp.int32)[None, :, None]
    inverse = jnp.sum(jnp.where(hit, iota[None, None, :], 0), axis=2).reshape(n_dp, n_dp, cap)
    present = jnp.any(hit, axis=2).reshape(n_dp, n_dp, cap)

    here = lax.dynamic_index_in_dim(inverse, mine, 1, keepdims=False)
    here_on = lax.dynamic_index_in_dim(present, mine, 1, keepdims=False)
    bins = jnp.arange(n_dp, dtype=jnp.int32)[:, None]
    home_nbr = idx[bins, here].reshape(homes)
    home_live = jnp.logical_and(here_on, live[bins, here]).astype(jnp.int32).reshape(homes)
    pair = (here // SLOTS * SLOTS)[:, :, None] + jnp.arange(SLOTS, dtype=jnp.int32)
    pair_spot = spot[bins[:, :, None], pair]
    pair_at = (pair_spot // cap * n_dp + bins[:, :, None]) * cap + pair_spot % cap
    pair_at = pair_at.astype(jnp.int32).reshape(homes * SLOTS)
    pair_on = live[bins[:, :, None], pair].astype(jnp.int32).reshape(homes * SLOTS)
    send_span = lax.dynamic_index_in_dim(inverse, mine, 0, keepdims=False).reshape(homes) // SLOTS
    my_spot = lax.dynamic_index_in_dim(spot, mine, 0, keepdims=False)
    my_live = lax.dynamic_index_in_dim(live, mine, 0, keepdims=False)

    def dispatch(x):
        chosen = jnp.take(x.reshape(spans, SPAN, hw), send_span, axis=0, mode="clip")
        return lax.all_to_all(chosen, "dp", split_axis=0, concat_axis=0, tiled=True)

    def collect(x):
        back = lax.all_to_all(x, "dp", split_axis=0, concat_axis=0, tiled=True)
        found = jnp.take(back, my_spot, axis=0, mode="clip")
        found = jnp.where(my_live[:, None, None], found.astype(F32), 0.0)
        return jnp.sum(found.reshape(spans, SLOTS, SPAN, hw), axis=1).astype(BF16).reshape(bin_rows, hw)

    def to_heads(x):
        split = x.reshape(group, piece_rows, n_f, hw).transpose(2, 0, 1, 3)
        return lax.all_to_all(split, "fsdp", split_axis=0, concat_axis=0, tiled=True)

    def to_rows(x):
        back = lax.all_to_all(x, "fsdp", split_axis=0, concat_axis=0, tiled=True)
        return back.transpose(1, 2, 0, 3).reshape(group, piece_rows, width)

    q_heads = lax.all_to_all(queries, "fsdp", split_axis=1, concat_axis=0, tiled=True)
    home_q = dispatch(q_heads)

    partial = dot(cotangent, out_proj, ((1,), (1,))).astype(BF16)
    parts = lax.all_to_all(
        partial.reshape(bin_rows, n_f, hw).transpose(1, 0, 2), "fsdp", split_axis=0, concat_axis=0, tiled=True
    )
    upstream = jnp.sum(parts.astype(F32), axis=0).astype(BF16)
    home_up = dispatch(upstream)

    keys = to_heads(nbr_keys)
    values = to_heads(nbr_values)

    slot_block = pl.BlockSpec((cap, SPAN, hw), lambda i, *_: (i, 0, 0))
    nbr_block = pl.BlockSpec((n_f, group, piece_rows, hw), lambda i, *_: (0, 0, 0, 0))
    stat_block = pl.BlockSpec((cap, 8, LANES), lambda i, *_: (i, 0, 0))
    params = pltpu.CompilerParams(vmem_limit_bytes=56 << 20)
    stats = pl.pallas_call(
        functools.partial(stats_kernel, heads, scale),
        grid_spec=pltpu.PrefetchScalarGridSpec(
            num_scalar_prefetch=2,
            grid=(n_dp,),
            in_specs=[slot_block, slot_block, nbr_block, nbr_block],
            out_specs=stat_block,
        ),
        out_shape=jax.ShapeDtypeStruct((homes, 8, LANES), F32),
        compiler_params=params,
    )(home_nbr, home_live, home_q, home_up, keys, values)
    all_stats = lax.all_gather(stats, "dp", axis=0, tiled=True)
    all_block = pl.BlockSpec((n_dp * homes, 8, LANES), lambda i, *_: (0, 0, 0))
    home_o, home_gq, grad_k, grad_v = pl.pallas_call(
        functools.partial(grads_kernel, heads, scale),
        grid_spec=pltpu.PrefetchScalarGridSpec(
            num_scalar_prefetch=4,
            grid=(n_dp,),
            in_specs=[all_block, slot_block, slot_block, nbr_block, nbr_block],
            out_specs=[slot_block, slot_block, nbr_block, nbr_block],
            scratch_shapes=[pltpu.VMEM((group, nbr_len, hw), F32), pltpu.VMEM((group, nbr_len, hw), F32)],
        ),
        out_shape=[
            jax.ShapeDtypeStruct((homes, SPAN, hw), BF16),
            jax.ShapeDtypeStruct((homes, SPAN, hw), BF16),
            jax.ShapeDtypeStruct((n_f, group, piece_rows, hw), BF16),
            jax.ShapeDtypeStruct((n_f, group, piece_rows, hw), BF16),
        ],
        compiler_params=params,
    )(home_nbr, home_live, pair_at, pair_on, all_stats, home_q, home_up, keys, values)

    attended_heads = collect(home_o)
    attended = lax.all_to_all(attended_heads, "fsdp", split_axis=0, concat_axis=1, tiled=True)
    grad_queries = lax.all_to_all(collect(home_gq), "fsdp", split_axis=0, concat_axis=1, tiled=True)
    grad_keys = to_rows(grad_k)
    grad_values = to_rows(grad_v)

    proj_cols = cotangent.shape[1]
    raw = (n_dp - 1) * bin_rows * (hw + proj_cols // n_e)
    summed = 2 * width * proj_cols * (n_dp - 1) // n_dp
    if raw <= summed and n_e == 2 and n_f % 2 == 0 and n_f & (n_f - 1) == 0:
        half = bin_rows // 2
        pieces = line_gather(lax.dynamic_slice_in_dim(cotangent, enc * half, half, 0), "dp")
        cots = [cotangent]
        for piece in pieces[1:]:
            other = swap(piece, "enc", 1)
            cots.append(jnp.where(enc == 0, piece, other))
            cots.append(jnp.where(enc == 0, other, piece))
        cot_all = jnp.concatenate(cots, axis=0)
        own = line_gather(attended_heads, "dp")
        grad_proj = jnp.zeros((width, proj_cols), BF16)
        for y in range(0, n_f, 2):
            even = own if y == 0 else [swap(piece, "fsdp", y) for piece in own]
            for bits, blocks in ((y, even), (y ^ 1, [swap(piece, "fsdp", 1) for piece in even])):
                term = dot(jnp.concatenate(blocks, axis=0), cot_all, ((0,), (0,))).astype(BF16)
                grad_proj = lax.dynamic_update_slice(grad_proj, term, ((place ^ bits) * hw, jnp.int32(0)))
    else:
        gathered = lax.all_gather(attended_heads, "fsdp", axis=1, tiled=True)
        grad_proj = lax.psum(dot(gathered, cotangent, ((0,), (0,))).astype(BF16), "dp")
    return (attended, grad_queries, grad_keys, grad_values, grad_proj)


def solution(mesh):
    placed = (
        P(("dp", "fsdp"), "enc"),
        P("dp", "fsdp", "enc"),
        P("dp", "fsdp", "enc"),
        P("enc", "fsdp"),
        P(),
        P(),
        P(),
        P("dp", "fsdp"),
    )
    return jax.shard_map(
        local,
        mesh=mesh,
        in_specs=placed,
        out_specs=(
            P(("dp", "fsdp"), "enc"),
            P(("dp", "fsdp"), "enc"),
            P("dp", "fsdp", "enc"),
            P("dp", "fsdp", "enc"),
            P("enc", "fsdp"),
        ),
        check_vma=False,
    )
```

```python
import functools
import math

import jax
import jax.numpy as jnp
from jax import lax
from jax.experimental import pallas as pl
from jax.experimental.pallas import tpu as pltpu
from jax.sharding import PartitionSpec as P

HEAD_DIM = 128
SPAN = 64
SLOTS = 2
LANES = 128
LOW = -1e30
BF16 = jnp.bfloat16
F32 = jnp.float32


def dot(a, b, dims):
    return lax.dot_general(a, b, ((dims[0], dims[1]), ((), ())), preferred_element_type=F32)


def neighbour_head(refs, n, cols):
    evens, odds = refs[:-1], refs[-1]
    return jnp.concatenate([x for k, ref in enumerate(evens) for x in (ref[n, :, cols], odds[k, n, :, cols])], axis=0)


def columns_of(rows):
    return jnp.concatenate([rows, jnp.zeros((LANES - rows.shape[0], LANES), F32)], axis=0).T


def joined_stats(heads, stats_ref, where_ref, on_ref, first):
    peaks, totals, weights = [], [], []
    for s in range(SLOTS):
        tile = stats_ref[where_ref[first + s]]
        on = on_ref[first + s] != 0
        peaks.append(jnp.where(on, tile[:heads, :SPAN], LOW))
        totals.append(jnp.where(on, tile[:heads, SPAN:], 0.0))
        weights.append(jnp.where(on, tile[heads : 2 * heads, :SPAN], 0.0))
    peak = functools.reduce(jnp.maximum, peaks)
    factors = [jnp.exp(p - peak) for p in peaks]
    shares = [f * t for f, t in zip(factors, totals)]
    return peak, factors, shares, weights


def index_kernel(n_dp, spans, cap, at_ref, src_ref, idx_ref, count_ref,
                 spot_ref, stat_ref, on_ref, nbr_ref, live_ref, span_ref, first_ref, send_ref, seen_ref):
    mine = at_ref[0]
    homes = n_dp * cap
    slots = spans * SLOTS

    def clear(j, carry):
        for ref in (nbr_ref, live_ref, span_ref, first_ref, send_ref):
            ref[j] = 0
        return carry

    lax.fori_loop(0, homes, clear, 0)

    def one_bin(b, carry):
        def reset(g, inner):
            seen_ref[g] = 0
            return inner

        lax.fori_loop(0, n_dp, reset, 0)

        def one_span(c, inner):
            count = count_ref[b * spans + c]
            for s in range(SLOTS):
                t = b * slots + c * SLOTS + s
                group = src_ref[b * spans + c, s]
                rank = seen_ref[group]
                seen_ref[group] = rank + 1
                on = (s < count).astype(jnp.int32)
                spot_ref[t] = group * cap + rank
                on_ref[t] = on
                stat_ref[t] = lax.rem(mine - group + n_dp, n_dp) * homes + b * cap + rank

                @pl.when(group == mine)
                def _(rank=rank, on=on, s=s):
                    j = b * cap + rank
                    nbr_ref[j] = idx_ref[b * spans + c, s]
                    live_ref[j] = on
                    span_ref[j] = c
                    first_ref[j] = b * slots + c * SLOTS

                @pl.when(b == mine)
                def _(group=group, rank=rank):
                    send_ref[group * cap + rank] = c

            return inner

        lax.fori_loop(0, spans, one_span, 0)
        return carry

    lax.fori_loop(0, n_dp, one_bin, 0)


def pick_kernel(per, at_ref, span_ref, *refs):
    parts, out_ref = refs[:-1], refs[-1]

    def one(j, carry):
        c = span_ref[j]
        if len(parts) == 1:
            out_ref[j] = parts[0][c]
        else:
            step = lax.div(c, per) ^ at_ref[1]
            for k, ref in enumerate(parts[:-1]):

                @pl.when(step == 2 * k)
                def _(ref=ref):
                    out_ref[j] = ref[lax.rem(c, per)]

            @pl.when(step % 2 == 1)
            def _():
                out_ref[j] = parts[-1][step // 2, lax.rem(c, per)]

        return carry

    lax.fori_loop(0, out_ref.shape[0], one, 0)


def forward_kernel(heads, scale, parts, nbr_ref, live_ref, q_ref, up_ref, *refs):
    k_refs, v_refs = refs[:parts], refs[parts : 2 * parts]
    o_ref, out_ref = refs[2 * parts :]
    lane = lax.broadcasted_iota(jnp.int32, (SPAN, LANES), 1)

    def slot(r, carry):
        n = nbr_ref[r]
        live = live_ref[r] != 0

        @pl.when(live)
        def _():
            first = jnp.zeros((SPAN, LANES), F32)
            second = jnp.zeros((SPAN, LANES), F32)
            for h in range(heads):
                cols = slice(h * HEAD_DIM, (h + 1) * HEAD_DIM)
                values = neighbour_head(v_refs, n, cols)
                scores = dot(q_ref[r, :, cols], neighbour_head(k_refs, n, cols), ((1,), (1,))) * scale
                dprobs = dot(up_ref[r, :, cols], values, ((1,), (1,)))
                peak = jnp.max(scores, axis=1, keepdims=True)
                expo = jnp.exp(scores - peak)
                total = jnp.sum(expo, axis=1, keepdims=True)
                weighted = jnp.sum(expo * dprobs, axis=1, keepdims=True)
                o_ref[r, :, cols] = (dot(expo.astype(BF16), values, ((1,), (0,))) / total).astype(BF16)
                first = jnp.where(lane == h, peak, first)
                first = jnp.where(lane == heads + h, weighted, first)
                second = jnp.where(lane == h, total, second)
            out_ref[r] = jnp.concatenate([first, second], axis=0).T[:8, :]

        @pl.when(jnp.logical_not(live))
        def _():
            out_ref[r] = jnp.zeros((8, LANES), F32)
            o_ref[r] = jnp.zeros(o_ref.shape[1:], BF16)

        return carry

    lax.fori_loop(0, q_ref.shape[0], slot, 0)


def backward_kernel(heads, scale, parts, at_ref, nbr_ref, live_ref, first_ref, where_ref, on_ref, stats_ref, q_ref, up_ref,
                    *refs):
    k_refs, v_refs = refs[:parts], refs[parts : 2 * parts]
    gq_ref, gk_ref, gv_ref, acc_k, acc_v = refs[2 * parts :]
    n_f, _, piece_rows, _ = gk_ref.shape

    acc_k[...] = jnp.zeros_like(acc_k)
    acc_v[...] = jnp.zeros_like(acc_v)

    def slot(r, carry):
        n = nbr_ref[r]
        live = live_ref[r] != 0

        @pl.when(live)
        def _():
            peak, factors, shares, weights = joined_stats(heads, stats_ref, where_ref, on_ref, first_ref[r])
            total = sum(shares)
            weighted = sum(f * w for f, w in zip(factors, weights))
            columns = columns_of(jnp.concatenate([peak + jnp.log(total), weighted / total], axis=1))
            for h in range(heads):
                cols = slice(h * HEAD_DIM, (h + 1) * HEAD_DIM)
                q, up = q_ref[r, :, cols], up_ref[r, :, cols]
                keys, values = neighbour_head(k_refs, n, cols), neighbour_head(v_refs, n, cols)
                scores = dot(q, keys, ((1,), (1,))) * scale
                dprobs = dot(up, values, ((1,), (1,)))
                probs = jnp.exp(scores - columns[:SPAN, h : h + 1])
                probs_b = probs.astype(BF16)
                dscores = (probs * (dprobs - columns[SPAN:, h : h + 1]) * scale).astype(BF16)
                acc_k[n, :, cols] += dot(dscores, q, ((0,), (0,)))
                acc_v[n, :, cols] += dot(probs_b, up, ((0,), (0,)))
                gq_ref[r, :, cols] = dot(dscores, keys, ((1,), (0,))).astype(BF16)

        @pl.when(jnp.logical_not(live))
        def _():
            gq_ref[r] = jnp.zeros(gq_ref.shape[1:], BF16)

        return carry

    lax.fori_loop(0, q_ref.shape[0], slot, 0)

    def neighbour(n, carry):
        for p in range(n_f):
            rows = slice(p * piece_rows, (p + 1) * piece_rows)
            gk_ref[at_ref[1] ^ p, n] = acc_k[n, rows, :].astype(BF16)
            gv_ref[at_ref[1] ^ p, n] = acc_v[n, rows, :].astype(BF16)
        return carry

    lax.fori_loop(0, acc_k.shape[0], neighbour, 0)


def join_kernel(heads, weighted, at_ref, spot_ref, on_ref, *refs):
    block_ref, out_ref = refs[-2:]
    spans = out_ref.shape[0]

    def span(c, carry):
        first = (at_ref[0] * spans + c) * SLOTS
        if weighted:
            _, _, shares, _ = joined_stats(heads, refs[1], refs[0], on_ref, first)
            total = sum(shares)
            columns = columns_of(jnp.concatenate([share / total for share in shares], axis=1))
        for h in range(heads):
            cols = slice(h * HEAD_DIM, (h + 1) * HEAD_DIM)
            joined = jnp.zeros((SPAN, HEAD_DIM), F32)
            for s in range(SLOTS):
                part = block_ref[spot_ref[first + s], :, cols].astype(F32)
                if weighted:
                    part = part * columns[s * SPAN : (s + 1) * SPAN, h : h + 1]
                joined += jnp.where(on_ref[first + s] != 0, part, 0.0)
            out_ref[c, :, cols] = joined.astype(BF16)
        return carry

    lax.fori_loop(0, spans, span, 0)


def line_steps(x, axis):
    n = lax.axis_size(axis)
    rise = [(i, i + 1) for i in range(n - 1)]
    fall = [(i + 1, i) for i in range(n - 1)]
    ups, downs = [x], [x]
    for _ in range(n - 1):
        ups.append(lax.ppermute(ups[-1], axis, rise))
        downs.append(lax.ppermute(downs[-1], axis, fall))
    return ups, downs


def line_pick(ups, downs, mine):
    first = jnp.where(mine == 0, downs[1], ups[1])
    second = jnp.where(mine == 0, downs[2], jnp.where(mine == 3, ups[2], downs[1]))
    inner = jnp.where(mine == 1, downs[2], ups[2])
    third = jnp.where(mine == 0, downs[3], jnp.where(mine == 3, ups[3], inner))
    return [ups[0], first, second, third]


def swap(x, axis, bits):
    return lax.ppermute(x, axis, [(i, i ^ bits) for i in range(lax.axis_size(axis))])


def shift(x, axis, by):
    n = lax.axis_size(axis)
    if by % n == 0:
        return x
    return lax.ppermute(x, axis, [(i, (i + by) % n) for i in range(n)])


def after(x, *others):
    return lax.optimization_barrier((x, *others))[0]


def local(queries, nbr_keys, nbr_values, out_proj, nbr_source, nbr_index, nbr_count, cotangent):
    n_dp, n_f, n_e = lax.axis_size("dp"), lax.axis_size("fsdp"), lax.axis_size("enc")
    token_rows, width = queries.shape
    hw = width // n_f
    heads = hw // HEAD_DIM
    spans_here = token_rows // SPAN
    spans = spans_here * n_f
    slots = spans * SLOTS
    cap = (spans_here * SLOTS + n_dp - 1) // n_dp * n_f
    group, piece_rows, _ = nbr_keys.shape
    nbr_len = piece_rows * n_f
    bin_rows = token_rows * n_f
    homes = n_dp * cap
    proj_cols = cotangent.shape[1]
    scale = 1.0 / math.sqrt(HEAD_DIM)
    mine = lax.axis_index("dp")
    place = lax.axis_index("fsdp")
    enc = lax.axis_index("enc")
    core = place % 2
    chip = place - core
    bits = range(n_f)
    at = jnp.stack([mine, place]).astype(jnp.int32)

    full = pl.BlockSpec(memory_space=pltpu.VMEM)
    smem = pl.BlockSpec(memory_space=pltpu.SMEM)

    def call(kernel, n_smem, outs, args, flops, scratch=()):
        single = not isinstance(outs, list)
        shapes = [outs] if single else outs
        specs = [smem if len(o.shape) == 1 else full for o in shapes]
        return pl.pallas_call(
            kernel,
            in_specs=[smem] * n_smem + [full] * (len(args) - n_smem),
            out_specs=specs[0] if single else specs,
            out_shape=outs,
            scratch_shapes=scratch,
            compiler_params=pltpu.CompilerParams(vmem_limit_bytes=56 << 20),
            cost_estimate=pl.CostEstimate(flops=flops, bytes_accessed=0, transcendentals=0),
        )(*args)

    def shape(*dims, dtype=BF16):
        return jax.ShapeDtypeStruct(dims, dtype)

    def exchange(x, dim, firsts=None):
        size = x.shape[dim] // n_f

        def cut(y, start, count=1):
            return lax.dynamic_slice_in_dim(y, start * size, count * size, dim)

        got = [swap(cut(x, chip ^ k, 2), "fsdp", k) for k in bits[2::2]]
        if firsts is not None:
            firsts.extend(got)
        odds = swap(jnp.stack([cut(x, place ^ 1)] + [cut(y, 1 - core) for y in got]), "fsdp", 1)
        return [cut(x, place)] + [cut(y, core) for y in got], odds

    def to_rows(evens, odds, rows):
        out = jnp.zeros(rows + (width,), BF16)
        for k in bits:
            start = (jnp.int32(0),) * len(rows) + ((place ^ k) * hw,)
            x = odds[k // 2] if k % 2 else evens[k // 2]
            out = lax.dynamic_update_slice(out, x.reshape(rows + (hw,)), start)
        return out

    def trade(x):
        return lax.all_to_all(x, "dp", split_axis=0, concat_axis=0, tiled=True)

    raw = (n_dp - 1) * bin_rows * (hw + proj_cols // n_e)
    summed = 2 * width * proj_cols * (n_dp - 1) // n_dp
    gather_rows = raw <= summed and n_e == 2 and n_dp == 4
    if gather_rows:
        half = bin_rows // 2
        c_ups, c_downs = line_steps(lax.dynamic_slice_in_dim(cotangent, enc * half, half, 0), "dp")

    i32 = jnp.int32
    spot, stat_at, on, nbr, live, span_at, first_at, send = call(
        functools.partial(index_kernel, n_dp, spans, cap),
        4,
        [shape(n_dp * slots, dtype=i32)] * 3 + [shape(homes, dtype=i32)] * 5,
        [at, nbr_source, nbr_index, nbr_count],
        1 << 30,
        [pltpu.SMEM((n_dp,), i32)],
    )

    arrived = []
    q_evens, q_odds = exchange(queries, 1, arrived)
    block = shape(homes, SPAN, hw)
    q_parts = [x.reshape(spans_here, SPAN, hw) for x in q_evens] + [q_odds.reshape(n_f // 2, spans_here, SPAN, hw)]
    q_send = call(functools.partial(pick_kernel, spans_here), 2, block, [at, send] + q_parts, 1 << 30)
    home_q = trade(q_send)

    def upstream_term(k, weights):
        rows = lax.dynamic_slice_in_dim(weights, (place ^ k) * hw, hw, 0)
        return dot(cotangent, rows, ((1,), (1,)))

    odd = {k: swap(upstream_term(k, out_proj).astype(BF16), "fsdp", 1) for k in reversed(bits[1::2])}
    late_proj = after(out_proj, q_send)
    pairs = {k: upstream_term(k, late_proj) + odd[k ^ 1].astype(F32) for k in reversed(bits[::2])}
    upstream = pairs[0]
    for k in bits[2::2]:
        upstream = upstream + swap(pairs[k].astype(BF16), "fsdp", k).astype(F32)
    upstream = upstream.astype(BF16)
    if gather_rows:
        upstream = after(upstream, c_ups[1], c_downs[1])
    up_send = call(
        functools.partial(pick_kernel, spans), 2, block, [at, send, upstream.reshape(spans, SPAN, hw)], 1 << 30
    )
    home_up = trade(up_send)

    key_steps = []
    k_evens, k_odds = exchange(after(nbr_keys, *arrived), 2, key_steps)
    v_evens, v_odds = exchange(after(nbr_values, *key_steps), 2)
    stored = [*k_evens, k_odds, *v_evens, v_odds]
    parts = n_f // 2 + 1

    home_o, stats = call(
        functools.partial(forward_kernel, heads, scale, parts),
        2,
        [block, shape(homes, 8, LANES, dtype=F32)],
        [nbr, live, home_q, home_up, *stored],
        15 << 30,
    )
    back_o = trade(home_o)
    all_stats = jnp.concatenate([shift(stats, "dp", d) for d in range(n_dp)], axis=0)
    if gather_rows:
        all_stats = after(all_stats, c_ups[2], c_downs[2])
    home_gq, grad_k, grad_v = call(
        functools.partial(backward_kernel, heads, scale, parts),
        6,
        [block] + [shape(n_f, group, piece_rows, hw)] * 2,
        [at, nbr, live, first_at, stat_at, on, all_stats, home_q, home_up, *stored],
        30 << 30,
        [pltpu.VMEM((group, nbr_len, hw), F32)] * 2,
    )
    att_heads = call(
        functools.partial(join_kernel, heads, True), 4, shape(spans, SPAN, hw),
        [at, spot, on, stat_at, all_stats, back_o], 4 << 30,
    ).reshape(bin_rows, hw)

    if gather_rows:
        a_ups, a_downs = line_steps(jnp.where(enc == 0, att_heads, jnp.roll(att_heads, half, 0)), "dp")
        att = line_pick(a_ups, a_downs, mine)
        cots = [jnp.where(enc == 0, cotangent, jnp.roll(cotangent, half, 0))]
        for x in line_pick(c_ups, c_downs, mine)[1:]:
            cots.append(jnp.concatenate([x, swap(x, "enc", 1)], axis=0))
        early_cot = jnp.concatenate(cots[:-1], axis=0)
        home_gq = after(home_gq, a_ups[1], a_downs[1])
        grad_proj = jnp.zeros((width, proj_cols), BF16)
        for y in bits[::2]:
            blocks = att if y == 0 else [swap(x, "fsdp", y) for x in att]
            early, last = jnp.concatenate(blocks[:-1], axis=0), blocks[-1]
            for k, early_k, last_k in ((y, early, last), (y ^ 1, swap(early, "fsdp", 1), swap(last, "fsdp", 1))):
                term = dot(early_k, early_cot, ((0,), (0,))) + dot(last_k, cots[-1], ((0,), (0,)))
                grad_proj = lax.dynamic_update_slice(grad_proj, term.astype(BF16), ((place ^ k) * hw, jnp.int32(0)))
    else:
        gathered = lax.all_gather(att_heads, "fsdp", axis=1, tiled=True)
        grad_proj = lax.psum(dot(gathered, cotangent, ((0,), (0,))).astype(BF16), "dp")
    attended = to_rows(*exchange(att_heads, 0), (token_rows,))
    k_firsts = []
    grad_keys = to_rows(*exchange(grad_k, 0, k_firsts), (group, piece_rows))
    grad_values = to_rows(*exchange(after(grad_v, *k_firsts), 0), (group, piece_rows))
    gq_heads = call(
        functools.partial(join_kernel, heads, False), 3, shape(spans, SPAN, hw), [at, spot, on, trade(home_gq)], 4 << 30
    ).reshape(bin_rows, hw)
    grad_queries = to_rows(*exchange(gq_heads, 0), (token_rows,))
    return (attended, grad_queries, grad_keys, grad_values, grad_proj)


def solution(mesh):
    placed = (
        P(("dp", "fsdp"), "enc"),
        P("dp", "fsdp", "enc"),
        P("dp", "fsdp", "enc"),
        P("enc", "fsdp"),
        P(),
        P(),
        P(),
        P("dp", "fsdp"),
    )
    return jax.shard_map(
        local,
        mesh=mesh,
        in_specs=placed,
        out_specs=(
            P(("dp", "fsdp"), "enc"),
            P(("dp", "fsdp"), "enc"),
            P("dp", "fsdp", "enc"),
            P("dp", "fsdp", "enc"),
            P("enc", "fsdp"),
        ),
        check_vma=False,
    )
```

```python
import functools
import math

import jax
import jax.numpy as jnp
from jax import lax
from jax.experimental import pallas as pl
from jax.experimental.pallas import tpu as pltpu
from jax.sharding import PartitionSpec as P

HEAD_DIM = 128
SPAN = 64
SLOTS = 2
LANES = 128
LOW = -1e30
OPT = dict(
    yh=0, gg="", ld=0, late=0, qg=0, kg="q_send", c2="", c3="", x1="home_q", x2="", up0="key", up1="home_o",
    up2="att", up3="stats", half=1, lk="a2a", lf=0, ok="a2a", gk="a2a", ag="a1", bar=3, frst=1, gv=1, bw="a1",
)
BF16 = jnp.bfloat16
F32 = jnp.float32


def dot(a, b, dims):
    return lax.dot_general(a, b, ((dims[0], dims[1]), ((), ())), preferred_element_type=F32)


def neighbour_head(refs, n, cols):
    evens, odds = refs[:-1], refs[-1]
    return jnp.concatenate([x for k, ref in enumerate(evens) for x in (ref[n, :, cols], odds[k, n, :, cols])], axis=0)


def columns_of(rows):
    return jnp.concatenate([rows, jnp.zeros((LANES - rows.shape[0], LANES), F32)], axis=0).T


def rows_of(columns):
    lane = lax.broadcasted_iota(jnp.int32, (SPAN, LANES), 1)
    table = jnp.zeros((SPAN, LANES), F32)
    for h, column in enumerate(columns):
        table = jnp.where(lane == h, column, table)
    return table.T[:8, :]


def index_kernel(n_dp, spans, cap, at_ref, src_ref, idx_ref, count_ref,
                 spot_ref, on_ref, nbr_ref, bin_ref, span_ref, send_ref, list_ref, size_ref, live_ref, seen_ref):
    mine = at_ref[0]
    slots = spans * SLOTS

    def clear(j, carry):
        for ref in (nbr_ref, live_ref, bin_ref, span_ref, send_ref, list_ref):
            ref[j] = 0
        return carry

    lax.fori_loop(0, n_dp * cap, clear, 0)

    def one_bin(b, carry):
        def reset(g, inner):
            seen_ref[g] = 0
            return inner

        lax.fori_loop(0, n_dp, reset, 0)

        def one_span(c, inner):
            count = count_ref[b * spans + c]
            for s in range(SLOTS):
                group = src_ref[b * spans + c, s]
                rank = seen_ref[group]
                seen_ref[group] = rank + 1
                on = (s < count).astype(jnp.int32)

                @pl.when(group == mine)
                def _(rank=rank, on=on, s=s):
                    j = b * cap + rank
                    nbr_ref[j] = idx_ref[b * spans + c, s]
                    live_ref[j] = on
                    bin_ref[j] = b
                    span_ref[j] = c

                @pl.when(b == mine)
                def _(group=group, rank=rank, on=on, s=s):
                    send_ref[group * cap + rank] = c
                    spot_ref[c * SLOTS + s] = group * cap + rank
                    on_ref[c * SLOTS + s] = on

            return inner

        lax.fori_loop(0, spans, one_span, 0)
        return carry

    lax.fori_loop(0, n_dp, one_bin, 0)

    def gather(j, size):
        @pl.when(live_ref[j] != 0)
        def _():
            list_ref[size] = j

        return size + live_ref[j]

    size = lax.fori_loop(0, n_dp * cap, gather, 0)
    size_ref[0] = size

    def fill(j, carry):
        @pl.when(jnp.logical_and(live_ref[j] == 0, size % 2 == 1))
        def _():
            list_ref[size] = j

        return carry

    lax.fori_loop(0, n_dp * cap, fill, 0)


def pick_kernel(per, at_ref, span_ref, *refs):
    parts, out_ref = refs[:-1], refs[-1]

    def one(j, carry):
        c = span_ref[j]
        if len(parts) == 1:
            out_ref[j] = parts[0][c]
        else:
            step = lax.div(c, per) ^ at_ref[1]
            for k, ref in enumerate(parts[:-1]):

                @pl.when(step == 2 * k)
                def _(ref=ref):
                    out_ref[j] = ref[lax.rem(c, per)]

            @pl.when(step % 2 == 1)
            def _():
                out_ref[j] = parts[-1][step // 2, lax.rem(c, per)]

        return carry

    lax.fori_loop(0, out_ref.shape[0], one, 0)


def forward_kernel(heads, scale, parts, nbr_ref, live_ref, size_ref, q_ref, *refs):
    k_refs, v_refs = refs[:parts], refs[parts : 2 * parts]
    o_ref, out_ref = refs[2 * parts :]

    def pair(i, carry):
        logs = [[], []]
        for h in range(heads):
            cols = slice(h * HEAD_DIM, (h + 1) * HEAD_DIM)
            for u in range(2):
                r = live_ref[2 * i + u]
                n = nbr_ref[r]
                scores = dot(q_ref[r, :, cols], neighbour_head(k_refs, n, cols), ((1,), (1,))) * scale
                peak = jnp.max(scores, axis=1, keepdims=True)
                expo = jnp.exp(scores - peak)
                total = jnp.sum(expo, axis=1, keepdims=True)
                part = dot(expo.astype(BF16), neighbour_head(v_refs, n, cols), ((1,), (0,)))
                o_ref[r, :, cols] = (part / total).astype(BF16)
                logs[u].append(peak + jnp.log(total))
        for u in range(2):
            out_ref[live_ref[2 * i + u]] = jnp.concatenate([rows_of(logs[u]), jnp.zeros((8, LANES - SPAN), F32)], axis=1)
        return carry

    lax.fori_loop(0, (size_ref[0] + 1) // 2, pair, 0)


def join_kernel(heads, n_dp, shifted, at_ref, spot_ref, on_ref, stats_ref, block_ref, up_ref, out_ref, turned_ref, send_ref):
    spans = out_ref.shape[0]
    cap = send_ref.shape[0] // n_dp
    send_ref[...] = jnp.zeros_like(send_ref)

    def span(c, carry):
        turned = lax.rem(c + at_ref[2], spans)
        spots = [spot_ref[c * SLOTS + s] for s in range(SLOTS)]
        on = [on_ref[c * SLOTS + s] != 0 for s in range(SLOTS)]
        came = spots
        if shifted:
            came = [lax.rem(at_ref[0] - lax.div(x, cap) + n_dp, n_dp) * cap + lax.rem(x, cap) for x in spots]
        logs = [jnp.where(o, stats_ref[x][:, :SPAN], LOW) for o, x in zip(on, came)]
        peak = functools.reduce(jnp.maximum, logs)
        expos = [jnp.exp(x - peak) for x in logs]
        total = sum(expos)
        columns = columns_of(jnp.concatenate([x / total for x in expos], axis=1))
        centres = []
        for h in range(heads):
            cols = slice(h * HEAD_DIM, (h + 1) * HEAD_DIM)
            joined = jnp.zeros((SPAN, HEAD_DIM), F32)
            for s in range(SLOTS):
                part = block_ref[spots[s], :, cols].astype(F32) * columns[s * SPAN : (s + 1) * SPAN, h : h + 1]
                joined += jnp.where(on[s], part, 0.0)
            out_ref[c, :, cols] = joined.astype(BF16)
            turned_ref[turned, :, cols] = joined.astype(BF16)
            centres.append(jnp.sum(joined * up_ref[turned, :, cols].astype(F32), axis=1, keepdims=True))
        tile = jnp.concatenate([peak + jnp.log(total), rows_of(centres)], axis=1)
        for s in range(SLOTS):
            send_ref[spots[s]] = tile
        return carry

    lax.fori_loop(0, spans, span, 0)


def backward_kernel(heads, scale, parts, at_ref, nbr_ref, live_ref, size_ref, upat_ref, stats_ref, q_ref, up_ref, *refs):
    k_refs, v_refs = refs[:parts], refs[parts : 2 * parts]
    gq_ref, gk_ref, gv_ref, acc_k, acc_v = refs[2 * parts :]
    n_f, _, piece_rows, _ = gk_ref.shape

    acc_k[...] = jnp.zeros_like(acc_k)
    acc_v[...] = jnp.zeros_like(acc_v)

    def pair(i, carry):
        at = [live_ref[2 * i + u] for u in range(2)]
        valid = [2 * i + u < size_ref[0] for u in range(2)]
        columns = [columns_of(stats_ref[r]) for r in at]
        for h in range(heads):
            cols = slice(h * HEAD_DIM, (h + 1) * HEAD_DIM)
            found = []
            for u, r in enumerate(at):
                n = nbr_ref[r]
                q, up = q_ref[r, :, cols], up_ref[upat_ref[r], :, cols]
                keys, values = neighbour_head(k_refs, n, cols), neighbour_head(v_refs, n, cols)
                scores = dot(q, keys, ((1,), (1,))) * scale
                dprobs = dot(up, values, ((1,), (1,)))
                probs = jnp.exp(scores - columns[u][:SPAN, h : h + 1])
                dscores = probs * (dprobs - columns[u][SPAN:, h : h + 1]) * scale
                probs_b = jnp.where(valid[u], probs, 0.0).astype(BF16)
                dscores = jnp.where(valid[u], dscores, 0.0).astype(BF16)
                gq_ref[r, :, cols] = dot(dscores, keys, ((1,), (0,))).astype(BF16)
                found.append((n, dot(dscores, q, ((0,), (0,))), dot(probs_b, up, ((0,), (0,)))))
            for n, key_part, value_part in found:
                acc_k[n, :, cols] += key_part
                acc_v[n, :, cols] += value_part
        return carry

    lax.fori_loop(0, (size_ref[0] + 1) // 2, pair, 0)

    def neighbour(n, carry):
        for p in range(n_f):
            rows = slice(p * piece_rows, (p + 1) * piece_rows)
            gk_ref[at_ref[1] ^ p, n] = acc_k[n, rows, :].astype(BF16)
            gv_ref[at_ref[1] ^ p, n] = acc_v[n, rows, :].astype(BF16)
        return carry

    lax.fori_loop(0, acc_k.shape[0], neighbour, 0)


def sum_kernel(spot_ref, on_ref, block_ref, out_ref):
    def span(c, carry):
        total = jnp.zeros(out_ref.shape[1:], F32)
        for s in range(SLOTS):
            at = c * SLOTS + s
            total += jnp.where(on_ref[at] != 0, block_ref[spot_ref[at]].astype(F32), 0.0)
        out_ref[c] = total.astype(BF16)
        return carry

    lax.fori_loop(0, out_ref.shape[0], span, 0)


def line_steps(x, axis, gates={}):
    ups, downs = [x], [x]
    for k in range(1, lax.axis_size(axis)):
        up, down = after((ups[-1], downs[-1]), *gates[k]) if k in gates else (ups[-1], downs[-1])
        up, down = line_last(up, down, axis)
        ups.append(up)
        downs.append(down)
    return ups, downs


def line_last(up, down, axis):
    n = lax.axis_size(axis)
    rise = [(i, i + 1) for i in range(n - 1)]
    fall = [(i + 1, i) for i in range(n - 1)]
    return lax.ppermute(up, axis, rise), lax.ppermute(down, axis, fall)


ORDER = ((0, 1, 2, 3), (1, 0, 2, 3), (2, 1, 3, 0), (3, 2, 1, 0))


def line_first_pick(up, down, mine):
    return jnp.where(mine == 0, down, up)


def line_pick(ups, downs, mine):
    first = line_first_pick(ups[1], downs[1], mine)
    ups2, downs2 = after((ups[2], downs[2]), first)
    second = jnp.where(mine == 0, downs2, jnp.where(mine == 3, ups2, downs[1]))
    inner = jnp.where(mine == 1, downs2, ups2)
    ups3, downs3 = after((ups[3], downs[3]), second)
    third = jnp.where(mine == 0, downs3, jnp.where(mine == 3, ups3, inner))
    return [ups[0], first, second, third]


def swap(x, axis, bits):
    return lax.ppermute(x, axis, [(i, i ^ bits) for i in range(lax.axis_size(axis))])


def shift(x, axis, by):
    n = lax.axis_size(axis)
    if by % n == 0:
        return x
    return lax.ppermute(x, axis, [(i, (i + by) % n) for i in range(n)])


def after(x, *others):
    return lax.optimization_barrier((x, *others))[0]


def local(queries, nbr_keys, nbr_values, out_proj, nbr_source, nbr_index, nbr_count, cotangent):
    n_dp, n_f, n_e = lax.axis_size("dp"), lax.axis_size("fsdp"), lax.axis_size("enc")
    token_rows, width = queries.shape
    hw = width // n_f
    heads = hw // HEAD_DIM
    spans_here = token_rows // SPAN
    spans = spans_here * n_f
    slots = spans * SLOTS
    cap = (spans_here * SLOTS + n_dp - 1) // n_dp * n_f
    group, piece_rows, _ = nbr_keys.shape
    nbr_len = piece_rows * n_f
    bin_rows = token_rows * n_f
    homes = n_dp * cap
    proj_cols = cotangent.shape[1]
    scale = 1.0 / math.sqrt(HEAD_DIM)
    mine = lax.axis_index("dp")
    place = lax.axis_index("fsdp")
    enc = lax.axis_index("enc")
    core = place % 2
    chip = place - core
    bits = range(n_f)
    half = bin_rows // 2
    raw = (n_dp - 1) * bin_rows * (hw + proj_cols // n_e)
    summed = 2 * width * proj_cols * (n_dp - 1) // n_dp
    gather_rows = raw <= summed and (n_e, n_dp, n_f) == (2, 4, 4) and half % SPAN == 0
    turn = enc * (spans // 2) if gather_rows else jnp.int32(0)
    at = jnp.stack([mine, place, turn]).astype(jnp.int32)

    full = pl.BlockSpec(memory_space=pltpu.VMEM)
    smem = pl.BlockSpec(memory_space=pltpu.SMEM)

    def call(kernel, n_smem, outs, args, flops, scratch=()):
        single = not isinstance(outs, list)
        shapes = [outs] if single else outs
        specs = [smem if len(o.shape) == 1 else full for o in shapes]
        return pl.pallas_call(
            kernel,
            in_specs=[smem] * n_smem + [full] * (len(args) - n_smem),
            out_specs=specs[0] if single else specs,
            out_shape=outs,
            scratch_shapes=scratch,
            compiler_params=pltpu.CompilerParams(vmem_limit_bytes=56 << 20),
            cost_estimate=pl.CostEstimate(flops=flops, bytes_accessed=0, transcendentals=0),
        )(*args)

    def shape(*dims, dtype=BF16):
        return jax.ShapeDtypeStruct(dims, dtype)

    def exchange(x, dim, firsts=None, gates=()):
        size = x.shape[dim] // n_f

        def cut(y, start, count=1):
            return lax.dynamic_slice_in_dim(y, start * size, count * size, dim)

        got = [swap(cut(x, chip ^ k, 2), "fsdp", k) for k in bits[2::2]]
        if firsts is not None:
            firsts.extend(got)
        if gates:
            x, got = after((x, got), *gates)
        odds = swap(jnp.stack([cut(x, place ^ 1)] + [cut(y, 1 - core) for y in got]), "fsdp", 1)
        return [cut(x, place)] + [cut(y, core) for y in got], odds

    def to_rows(evens, odds, rows):
        out = jnp.zeros(rows + (width,), BF16)
        for k in bits:
            start = (jnp.int32(0),) * len(rows) + ((place ^ k) * hw,)
            x = odds[k // 2] if k % 2 else evens[k // 2]
            out = lax.dynamic_update_slice(out, x.reshape(rows + (hw,)), start)
        return out

    def trade(x, kind="a2a", sign=1):
        if kind == "a2a":
            return lax.all_to_all(x, "dp", split_axis=0, concat_axis=0, tiled=True)
        to = x.reshape((n_dp, -1) + x.shape[1:])
        got = [shift(lax.dynamic_index_in_dim(to, (mine + r) % n_dp, 0, keepdims=False), "dp", r) for r in range(n_dp)]
        out = jnp.zeros_like(to)
        for r, y in enumerate(got):
            out = lax.dynamic_update_index_in_dim(out, y, (mine - r) % n_dp, 0)
        return out.reshape(x.shape)

    i32 = jnp.int32
    spot, on, nbr, bin_at, span_at, send, live, live_count = call(
        functools.partial(index_kernel, n_dp, spans, cap),
        4,
        [shape(slots, dtype=i32)] * 2 + [shape(homes, dtype=i32)] * 5 + [shape(1, dtype=i32)],
        [at, nbr_source, nbr_index, nbr_count],
        1 << 30,
        [pltpu.SMEM((homes,), i32), pltpu.SMEM((n_dp,), i32)],
    )

    q_evens, q_odds = exchange(queries, 1, None, [send] if OPT["qg"] else ())
    block = shape(homes, SPAN, hw)
    q_parts = [x.reshape(spans_here, SPAN, hw) for x in q_evens] + [q_odds.reshape(n_f // 2, spans_here, SPAN, hw)]
    q_send = call(functools.partial(pick_kernel, spans_here), 2, block, [at, send] + q_parts, 1 << 30)
    home_q = trade(q_send)

    if gather_rows:
        own_half = lax.dynamic_slice_in_dim(cotangent, enc * half, half, 0)
        c_ups, c_downs = line_steps(own_half, "dp", {2: [home_q]} if OPT["c2"] else {})


    key_steps = []
    k_evens, k_odds = exchange(after(nbr_keys, q_send if OPT["kg"] == "q_send" else q_odds), 2, key_steps)
    line_first = [c_ups[1], c_downs[1]] if gather_rows else []
    v_evens, v_odds = exchange(after(nbr_values, *key_steps, *line_first), 2)
    stored = [*k_evens, k_odds, *v_evens, v_odds]
    parts = n_f // 2 + 1

    marks = {"": [], "key": key_steps, "q_send": [q_send], "home_q": [home_q]}
    i32 = jnp.int32
    tiles = shape(homes, 8, LANES, dtype=F32)
    home_o, home_logs = call(
        functools.partial(forward_kernel, heads, scale, parts),
        3,
        [block, tiles],
        [nbr, live, live_count, home_q, *stored],
        12 << 30,
    )
    marks["home_o"] = [home_o]
    logs_to = home_logs.reshape(n_dp, cap, 8, LANES)
    if OPT["lk"] == "shift":
        back_logs = jnp.concatenate(
            [shift(lax.dynamic_index_in_dim(logs_to, (mine + r) % n_dp, 0, keepdims=False), "dp", r) for r in range(n_dp)]
        )
    else:
        back_logs = trade(home_logs)
    marks["logs"] = [back_logs]
    back_o = trade(after(home_o, back_logs) if OPT["lf"] else home_o, OPT["ok"], -1)

    def gate(x, name):
        return after(x, *marks[OPT[name]]) if marks[OPT[name]] else x

    late_cot, late_proj = gate((cotangent, out_proj), "up0")
    cots = [late_cot]
    if gather_rows:
        cots = [jnp.where(enc == 0, late_cot, jnp.roll(late_cot, half, 0))]
        first = line_first_pick(*gate((c_ups[1], c_downs[1]), "x1"), mine)
        halves = [(first, swap(first, "enc", 1))]
        c_ups[3], c_downs[3] = line_last(*gate((c_ups[2], c_downs[2]), "c3"), "dp")
        c_ups[2], c_downs[2] = gate((c_ups[2], c_downs[2]), "x2")
        halves += [(x, swap(x, "enc", 1)) for x in line_pick(c_ups, c_downs, mine)[2:]]

    def proj_rows(k):
        return lax.dynamic_slice_in_dim(late_proj, (place ^ k) * hw, hw, 0)

    even_rows = jnp.concatenate([proj_rows(k) for k in bits[::2]], axis=0)
    odd_rows = jnp.concatenate([proj_rows(k) for k in bits[1::2]], axis=0)

    def upstream_of(cot):
        given = swap(dot(cot, odd_rows, ((1,), (1,))).astype(BF16), "fsdp", 1)
        pair = dot(cot, even_rows, ((1,), (1,))) + given.astype(F32)
        total = pair[:, :hw]
        for k in bits[2::2]:
            total += swap(pair[:, k // 2 * hw : (k // 2 + 1) * hw].astype(BF16), "fsdp", k).astype(F32)
        return total.astype(BF16).reshape(-1, SPAN, hw)

    ups = [upstream_of(cots[0])]
    if gather_rows and OPT["up1"] != "att":
        cots.append(jnp.concatenate(gate(halves[0], "up1"), axis=0))
        ups.append(upstream_of(cots[1]))
    if gather_rows and OPT["up1"] != "att" and OPT["up2"] != "att":
        cots.append(jnp.concatenate(gate(halves[1], "up2"), axis=0))
        ups.append(upstream_of(cots[2]))
    heads_of_bin = shape(spans, SPAN, hw)
    att_heads, att_turned, stats = call(
        functools.partial(join_kernel, heads, n_dp, OPT["lk"] == "shift"), 3, [heads_of_bin, heads_of_bin, tiles],
        [at, spot, on, back_logs, back_o, ups[0]], 5 << 30,
    )
    att_heads, att_turned = att_heads.reshape(bin_rows, hw), att_turned.reshape(bin_rows, hw)
    home_stats = trade(stats)
    if gather_rows:
        payload = att_turned
        if OPT["yh"]:
            payload = jnp.concatenate([att_turned, swap(att_turned[:, : hw // 2], "fsdp", 2)], axis=1)
        a_ups, a_downs = line_steps(payload, "dp")
        marks["att"], marks["stats"] = [att_turned], [home_stats]
        for k in range(len(cots), 3):
            cots.append(jnp.concatenate(after(halves[k - 1], att_turned), axis=0))
            ups.append(upstream_of(cots[k]))
        last_half = gate(halves[2], "up3")
        cots.append(jnp.concatenate(last_half, axis=0))
        ups += [upstream_of(x) for x in last_half] if OPT["half"] else [upstream_of(cots[3])]
        step_of = jnp.array([[order.index(b) for b in range(4)] for order in ORDER], i32)[mine]
        home_up = jnp.concatenate(ups, axis=0)
        up_at = step_of[bin_at] * spans + (span_at + turn) % spans
        hop = 2 if OPT["ag"] == "a2" else 1
        late_att, late_first = after((att_heads, payload), home_stats, a_ups[hop], a_downs[hop])
        hop = 2 if OPT["bw"] == "a2" else 1
        home_stats = after(home_stats, a_ups[hop], a_downs[hop])
    else:
        home_up = trade(call(functools.partial(pick_kernel, spans), 2, block, [at, send, ups[0]], 1 << 30))
        up_at = jnp.arange(homes, dtype=i32)
        late_att = att_heads
    home_gq, grad_k, grad_v = call(
        functools.partial(backward_kernel, heads, scale, parts),
        5,
        [block] + [shape(n_f, group, piece_rows, hw)] * 2,
        [at, nbr, live, live_count, up_at, home_stats, home_q, home_up, *stored],
        30 << 30,
        [pltpu.VMEM((group, nbr_len, hw), F32)] * 2,
    )

    firsts = []
    att_evens, att_odds = exchange(late_att, 0, firsts)
    if gather_rows:
        att = line_pick(a_ups, a_downs, mine)
        bar = OPT["bar"]

        def cross(x):
            return swap(x[:, hw // 2 : hw] if OPT["yh"] else x, "fsdp", 2)

        crossed = [cross(x) for x in ([late_first] + att[1:])[:bar]]
        if OPT["frst"]:
            firsts = lax.optimization_barrier((firsts, home_gq))[0]
            home_gq, grad_k, grad_v = after((home_gq, grad_k, grad_v), *firsts)
        keep = min(bar + 1, 4)
        home_gq, grad_k, grad_v, att[:keep], crossed = lax.optimization_barrier(
            (home_gq, grad_k, grad_v, att[:keep], crossed)
        )
        if OPT["gg"] == "a3":
            home_gq = after(home_gq, a_ups[3], a_downs[3])
        if OPT["late"]:
            att[bar:] = after(att[bar:], home_gq)
        crossed += [cross(x) for x in att[bar:]]
        far = [jnp.concatenate([x[:, hw:], y], axis=1) for x, y in zip(att, crossed)] if OPT["yh"] else crossed
        near = [x[:, :hw] for x in att] if OPT["yh"] else att
        early_cot = jnp.concatenate(cots[:-1], axis=0)
        grad_proj = jnp.zeros((width, proj_cols), BF16)
        for k, blocks in ((0, near), (2, far)):
            early, last = jnp.concatenate(blocks[:-1], axis=0), blocks[-1]
            for bit, early_k, last_k in ((k, early, last), (k ^ 1, swap(early, "fsdp", 1), swap(last, "fsdp", 1))):
                if OPT["ld"]:
                    early_k = after(early_k, last_k)
                term = dot(early_k, early_cot, ((0,), (0,))) + dot(last_k, cots[-1], ((0,), (0,)))
                grad_proj = lax.dynamic_update_slice(grad_proj, term.astype(BF16), ((place ^ bit) * hw, jnp.int32(0)))
    else:
        gathered = lax.all_gather(att_heads, "fsdp", axis=1, tiled=True)
        grad_proj = lax.psum(dot(gathered, cotangent, ((0,), (0,))).astype(BF16), "dp")
    firsts = []
    grad_keys = to_rows(*exchange(grad_k, 0, firsts), (group, piece_rows))
    grad_values = to_rows(*exchange(after(grad_v, *firsts) if OPT["gv"] else grad_v, 0), (group, piece_rows))
    attended = to_rows(att_evens, att_odds, (token_rows,))
    gq_heads = call(sum_kernel, 2, heads_of_bin, [spot, on, trade(home_gq, OPT["gk"], -1)], 3 << 30).reshape(bin_rows, hw)
    grad_queries = to_rows(*exchange(gq_heads, 0), (token_rows,))
    return (attended, grad_queries, grad_keys, grad_values, grad_proj)


def solution(mesh):
    placed = (
        P(("dp", "fsdp"), "enc"),
        P("dp", "fsdp", "enc"),
        P("dp", "fsdp", "enc"),
        P("enc", "fsdp"),
        P(),
        P(),
        P(),
        P("dp", "fsdp"),
    )
    return jax.shard_map(
        local,
        mesh=mesh,
        in_specs=placed,
        out_specs=(
            P(("dp", "fsdp"), "enc"),
            P(("dp", "fsdp"), "enc"),
            P("dp", "fsdp", "enc"),
            P("dp", "fsdp", "enc"),
            P("enc", "fsdp"),
        ),
        check_vma=False,
    )
```

```python
import functools
import math

import jax
import jax.numpy as jnp
from jax import lax
from jax.experimental import pallas as pl
from jax.experimental.pallas import tpu as pltpu
from jax.sharding import PartitionSpec as P

HEAD_DIM = 128
SPAN = 64
SLOTS = 2
LANES = 128
LOW = -1e30
OPT = dict(
    yh=0, gg="", ld=0, late=0, qg=0, kg="q_send", c2="", c3="", x1="home_q", x2="", up0="key", up1="home_o",
    up2="att", up3="stats", half=1, lk="a2a", lf=0, ok="a2a", gk="a2a", ag="a1", bar=3, frst=0, gv=1, bw="a1", yg=2,
)
BF16 = jnp.bfloat16
F32 = jnp.float32


def dot(a, b, dims):
    return lax.dot_general(a, b, ((dims[0], dims[1]), ((), ())), preferred_element_type=F32)


def neighbour_head(refs, n, cols):
    evens, odds = refs[:-1], refs[-1]
    return jnp.concatenate([x for k, ref in enumerate(evens) for x in (ref[n, :, cols], odds[k, n, :, cols])], axis=0)


def columns_of(rows):
    return jnp.concatenate([rows, jnp.zeros((LANES - rows.shape[0], LANES), F32)], axis=0).T


def rows_of(columns):
    lane = lax.broadcasted_iota(jnp.int32, (SPAN, LANES), 1)
    table = jnp.zeros((SPAN, LANES), F32)
    for h, column in enumerate(columns):
        table = jnp.where(lane == h, column, table)
    return table.T[:8, :]


def index_kernel(n_dp, spans, cap, at_ref, src_ref, idx_ref, count_ref,
                 spot_ref, on_ref, nbr_ref, bin_ref, span_ref, send_ref, list_ref, size_ref, live_ref, seen_ref):
    mine = at_ref[0]
    slots = spans * SLOTS

    def clear(j, carry):
        for ref in (nbr_ref, live_ref, bin_ref, span_ref, send_ref, list_ref):
            ref[j] = 0
        return carry

    lax.fori_loop(0, n_dp * cap, clear, 0)

    def one_bin(b, carry):
        def reset(g, inner):
            seen_ref[g] = 0
            return inner

        lax.fori_loop(0, n_dp, reset, 0)

        def one_span(c, inner):
            count = count_ref[b * spans + c]
            for s in range(SLOTS):
                group = src_ref[b * spans + c, s]
                rank = seen_ref[group]
                seen_ref[group] = rank + 1
                on = (s < count).astype(jnp.int32)

                @pl.when(group == mine)
                def _(rank=rank, on=on, s=s):
                    j = b * cap + rank
                    nbr_ref[j] = idx_ref[b * spans + c, s]
                    live_ref[j] = on
                    bin_ref[j] = b
                    span_ref[j] = c

                @pl.when(b == mine)
                def _(group=group, rank=rank, on=on, s=s):
                    send_ref[group * cap + rank] = c
                    spot_ref[c * SLOTS + s] = group * cap + rank
                    on_ref[c * SLOTS + s] = on

            return inner

        lax.fori_loop(0, spans, one_span, 0)
        return carry

    lax.fori_loop(0, n_dp, one_bin, 0)

    def gather(j, size):
        @pl.when(live_ref[j] != 0)
        def _():
            list_ref[size] = j

        return size + live_ref[j]

    size = lax.fori_loop(0, n_dp * cap, gather, 0)
    size_ref[0] = size

    def fill(j, carry):
        @pl.when(jnp.logical_and(live_ref[j] == 0, size % 2 == 1))
        def _():
            list_ref[size] = j

        return carry

    lax.fori_loop(0, n_dp * cap, fill, 0)


def pick_kernel(per, at_ref, span_ref, *refs):
    parts, out_ref = refs[:-1], refs[-1]

    def one(j, carry):
        c = span_ref[j]
        if len(parts) == 1:
            out_ref[j] = parts[0][c]
        else:
            step = lax.div(c, per) ^ at_ref[1]
            for k, ref in enumerate(parts[:-1]):

                @pl.when(step == 2 * k)
                def _(ref=ref):
                    out_ref[j] = ref[lax.rem(c, per)]

            @pl.when(step % 2 == 1)
            def _():
                out_ref[j] = parts[-1][step // 2, lax.rem(c, per)]

        return carry

    lax.fori_loop(0, out_ref.shape[0], one, 0)


def forward_kernel(heads, scale, parts, nbr_ref, live_ref, size_ref, q_ref, *refs):
    k_refs, v_refs = refs[:parts], refs[parts : 2 * parts]
    o_ref, out_ref = refs[2 * parts :]

    def pair(i, carry):
        logs = [[], []]
        for h in range(heads):
            cols = slice(h * HEAD_DIM, (h + 1) * HEAD_DIM)
            for u in range(2):
                r = live_ref[2 * i + u]
                n = nbr_ref[r]
                scores = dot(q_ref[r, :, cols], neighbour_head(k_refs, n, cols), ((1,), (1,))) * scale
                peak = jnp.max(scores, axis=1, keepdims=True)
                expo = jnp.exp(scores - peak)
                total = jnp.sum(expo, axis=1, keepdims=True)
                part = dot(expo.astype(BF16), neighbour_head(v_refs, n, cols), ((1,), (0,)))
                o_ref[r, :, cols] = (part / total).astype(BF16)
                logs[u].append(peak + jnp.log(total))
        for u in range(2):
            out_ref[live_ref[2 * i + u]] = jnp.concatenate([rows_of(logs[u]), jnp.zeros((8, LANES - SPAN), F32)], axis=1)
        return carry

    lax.fori_loop(0, (size_ref[0] + 1) // 2, pair, 0)


def join_kernel(heads, n_dp, shifted, at_ref, spot_ref, on_ref, stats_ref, block_ref, up_ref, out_ref, turned_ref, send_ref):
    spans = out_ref.shape[0]
    cap = send_ref.shape[0] // n_dp
    send_ref[...] = jnp.zeros_like(send_ref)

    def span(c, carry):
        turned = lax.rem(c + at_ref[2], spans)
        spots = [spot_ref[c * SLOTS + s] for s in range(SLOTS)]
        on = [on_ref[c * SLOTS + s] != 0 for s in range(SLOTS)]
        came = spots
        if shifted:
            came = [lax.rem(at_ref[0] - lax.div(x, cap) + n_dp, n_dp) * cap + lax.rem(x, cap) for x in spots]
        logs = [jnp.where(o, stats_ref[x][:, :SPAN], LOW) for o, x in zip(on, came)]
        peak = functools.reduce(jnp.maximum, logs)
        expos = [jnp.exp(x - peak) for x in logs]
        total = sum(expos)
        columns = columns_of(jnp.concatenate([x / total for x in expos], axis=1))
        centres = []
        for h in range(heads):
            cols = slice(h * HEAD_DIM, (h + 1) * HEAD_DIM)
            joined = jnp.zeros((SPAN, HEAD_DIM), F32)
            for s in range(SLOTS):
                part = block_ref[spots[s], :, cols].astype(F32) * columns[s * SPAN : (s + 1) * SPAN, h : h + 1]
                joined += jnp.where(on[s], part, 0.0)
            out_ref[c, :, cols] = joined.astype(BF16)
            turned_ref[turned, :, cols] = joined.astype(BF16)
            centres.append(jnp.sum(joined * up_ref[turned, :, cols].astype(F32), axis=1, keepdims=True))
        tile = jnp.concatenate([peak + jnp.log(total), rows_of(centres)], axis=1)
        for s in range(SLOTS):
            send_ref[spots[s]] = tile
        return carry

    lax.fori_loop(0, spans, span, 0)


def backward_kernel(heads, scale, parts, at_ref, nbr_ref, live_ref, size_ref, upat_ref, stats_ref, q_ref, up_ref, *refs):
    k_refs, v_refs = refs[:parts], refs[parts : 2 * parts]
    gq_ref, gk_ref, gv_ref, acc_k, acc_v = refs[2 * parts :]
    n_f, _, piece_rows, _ = gk_ref.shape

    acc_k[...] = jnp.zeros_like(acc_k)
    acc_v[...] = jnp.zeros_like(acc_v)

    def pair(i, carry):
        at = [live_ref[2 * i + u] for u in range(2)]
        valid = [2 * i + u < size_ref[0] for u in range(2)]
        columns = [columns_of(stats_ref[r]) for r in at]
        for h in range(heads):
            cols = slice(h * HEAD_DIM, (h + 1) * HEAD_DIM)
            found = []
            for u, r in enumerate(at):
                n = nbr_ref[r]
                q, up = q_ref[r, :, cols], up_ref[upat_ref[r], :, cols]
                keys, values = neighbour_head(k_refs, n, cols), neighbour_head(v_refs, n, cols)
                scores = dot(q, keys, ((1,), (1,))) * scale
                dprobs = dot(up, values, ((1,), (1,)))
                probs = jnp.exp(scores - columns[u][:SPAN, h : h + 1])
                dscores = probs * (dprobs - columns[u][SPAN:, h : h + 1]) * scale
                probs_b = jnp.where(valid[u], probs, 0.0).astype(BF16)
                dscores = jnp.where(valid[u], dscores, 0.0).astype(BF16)
                gq_ref[r, :, cols] = dot(dscores, keys, ((1,), (0,))).astype(BF16)
                found.append((n, dot(dscores, q, ((0,), (0,))), dot(probs_b, up, ((0,), (0,)))))
            for n, key_part, value_part in found:
                acc_k[n, :, cols] += key_part
                acc_v[n, :, cols] += value_part
        return carry

    lax.fori_loop(0, (size_ref[0] + 1) // 2, pair, 0)

    def neighbour(n, carry):
        for p in range(n_f):
            rows = slice(p * piece_rows, (p + 1) * piece_rows)
            gk_ref[at_ref[1] ^ p, n] = acc_k[n, rows, :].astype(BF16)
            gv_ref[at_ref[1] ^ p, n] = acc_v[n, rows, :].astype(BF16)
        return carry

    lax.fori_loop(0, acc_k.shape[0], neighbour, 0)


def sum_kernel(spot_ref, on_ref, block_ref, out_ref):
    def span(c, carry):
        total = jnp.zeros(out_ref.shape[1:], F32)
        for s in range(SLOTS):
            at = c * SLOTS + s
            total += jnp.where(on_ref[at] != 0, block_ref[spot_ref[at]].astype(F32), 0.0)
        out_ref[c] = total.astype(BF16)
        return carry

    lax.fori_loop(0, out_ref.shape[0], span, 0)


def line_steps(x, axis, gates={}):
    ups, downs = [x], [x]
    for k in range(1, lax.axis_size(axis)):
        up, down = after((ups[-1], downs[-1]), *gates[k]) if k in gates else (ups[-1], downs[-1])
        up, down = line_last(up, down, axis)
        ups.append(up)
        downs.append(down)
    return ups, downs


def line_last(up, down, axis):
    n = lax.axis_size(axis)
    rise = [(i, i + 1) for i in range(n - 1)]
    fall = [(i + 1, i) for i in range(n - 1)]
    return lax.ppermute(up, axis, rise), lax.ppermute(down, axis, fall)


ORDER = ((0, 1, 2, 3), (1, 0, 2, 3), (2, 1, 3, 0), (3, 2, 1, 0))


def line_first_pick(up, down, mine):
    return jnp.where(mine == 0, down, up)


def line_pick(ups, downs, mine):
    first = line_first_pick(ups[1], downs[1], mine)
    ups2, downs2 = after((ups[2], downs[2]), first)
    second = jnp.where(mine == 0, downs2, jnp.where(mine == 3, ups2, downs[1]))
    inner = jnp.where(mine == 1, downs2, ups2)
    ups3, downs3 = after((ups[3], downs[3]), second)
    third = jnp.where(mine == 0, downs3, jnp.where(mine == 3, ups3, inner))
    return [ups[0], first, second, third]


def swap(x, axis, bits):
    return lax.ppermute(x, axis, [(i, i ^ bits) for i in range(lax.axis_size(axis))])


def shift(x, axis, by):
    n = lax.axis_size(axis)
    if by % n == 0:
        return x
    return lax.ppermute(x, axis, [(i, (i + by) % n) for i in range(n)])


def after(x, *others):
    return lax.optimization_barrier((x, *others))[0]


def local(queries, nbr_keys, nbr_values, out_proj, nbr_source, nbr_index, nbr_count, cotangent):
    n_dp, n_f, n_e = lax.axis_size("dp"), lax.axis_size("fsdp"), lax.axis_size("enc")
    token_rows, width = queries.shape
    hw = width // n_f
    heads = hw // HEAD_DIM
    spans_here = token_rows // SPAN
    spans = spans_here * n_f
    slots = spans * SLOTS
    cap = (spans_here * SLOTS + n_dp - 1) // n_dp * n_f
    group, piece_rows, _ = nbr_keys.shape
    nbr_len = piece_rows * n_f
    bin_rows = token_rows * n_f
    homes = n_dp * cap
    proj_cols = cotangent.shape[1]
    scale = 1.0 / math.sqrt(HEAD_DIM)
    mine = lax.axis_index("dp")
    place = lax.axis_index("fsdp")
    enc = lax.axis_index("enc")
    core = place % 2
    chip = place - core
    bits = range(n_f)
    half = bin_rows // 2
    raw = (n_dp - 1) * bin_rows * (hw + proj_cols // n_e)
    summed = 2 * width * proj_cols * (n_dp - 1) // n_dp
    gather_rows = raw <= summed and (n_e, n_dp, n_f) == (2, 4, 4) and half % SPAN == 0
    turn = enc * (spans // 2) if gather_rows else jnp.int32(0)
    at = jnp.stack([mine, place, turn]).astype(jnp.int32)

    full = pl.BlockSpec(memory_space=pltpu.VMEM)
    smem = pl.BlockSpec(memory_space=pltpu.SMEM)

    def call(kernel, n_smem, outs, args, flops, scratch=()):
        single = not isinstance(outs, list)
        shapes = [outs] if single else outs
        specs = [smem if len(o.shape) == 1 else full for o in shapes]
        return pl.pallas_call(
            kernel,
            in_specs=[smem] * n_smem + [full] * (len(args) - n_smem),
            out_specs=specs[0] if single else specs,
            out_shape=outs,
            scratch_shapes=scratch,
            compiler_params=pltpu.CompilerParams(vmem_limit_bytes=56 << 20),
            cost_estimate=pl.CostEstimate(flops=flops, bytes_accessed=0, transcendentals=0),
        )(*args)

    def shape(*dims, dtype=BF16):
        return jax.ShapeDtypeStruct(dims, dtype)

    def exchange(x, dim, firsts=None, gates=()):
        size = x.shape[dim] // n_f

        def cut(y, start, count=1):
            return lax.dynamic_slice_in_dim(y, start * size, count * size, dim)

        got = [swap(cut(x, chip ^ k, 2), "fsdp", k) for k in bits[2::2]]
        if firsts is not None:
            firsts.extend(got)
        if gates:
            x, got = after((x, got), *gates)
        odds = swap(jnp.stack([cut(x, place ^ 1)] + [cut(y, 1 - core) for y in got]), "fsdp", 1)
        return [cut(x, place)] + [cut(y, core) for y in got], odds

    def to_rows(evens, odds, rows):
        out = jnp.zeros(rows + (width,), BF16)
        for k in bits:
            start = (jnp.int32(0),) * len(rows) + ((place ^ k) * hw,)
            x = odds[k // 2] if k % 2 else evens[k // 2]
            out = lax.dynamic_update_slice(out, x.reshape(rows + (hw,)), start)
        return out

    def trade(x, kind="a2a", sign=1):
        if kind == "a2a":
            return lax.all_to_all(x, "dp", split_axis=0, concat_axis=0, tiled=True)
        to = x.reshape((n_dp, -1) + x.shape[1:])
        got = [shift(lax.dynamic_index_in_dim(to, (mine + r) % n_dp, 0, keepdims=False), "dp", r) for r in range(n_dp)]
        out = jnp.zeros_like(to)
        for r, y in enumerate(got):
            out = lax.dynamic_update_index_in_dim(out, y, (mine - r) % n_dp, 0)
        return out.reshape(x.shape)

    i32 = jnp.int32
    spot, on, nbr, bin_at, span_at, send, live, live_count = call(
        functools.partial(index_kernel, n_dp, spans, cap),
        4,
        [shape(slots, dtype=i32)] * 2 + [shape(homes, dtype=i32)] * 5 + [shape(1, dtype=i32)],
        [at, nbr_source, nbr_index, nbr_count],
        1 << 30,
        [pltpu.SMEM((homes,), i32), pltpu.SMEM((n_dp,), i32)],
    )

    q_evens, q_odds = exchange(queries, 1, None, [send] if OPT["qg"] else ())
    block = shape(homes, SPAN, hw)
    q_parts = [x.reshape(spans_here, SPAN, hw) for x in q_evens] + [q_odds.reshape(n_f // 2, spans_here, SPAN, hw)]
    q_send = call(functools.partial(pick_kernel, spans_here), 2, block, [at, send] + q_parts, 1 << 30)
    home_q = trade(q_send)

    if gather_rows:
        own_half = lax.dynamic_slice_in_dim(cotangent, enc * half, half, 0)
        c_ups, c_downs = line_steps(own_half, "dp", {2: [home_q]} if OPT["c2"] else {})


    key_steps = []
    k_evens, k_odds = exchange(after(nbr_keys, q_send if OPT["kg"] == "q_send" else q_odds), 2, key_steps)
    line_first = [c_ups[1], c_downs[1]] if gather_rows else []
    v_evens, v_odds = exchange(after(nbr_values, *key_steps, *line_first), 2)
    stored = [*k_evens, k_odds, *v_evens, v_odds]
    parts = n_f // 2 + 1

    marks = {"": [], "key": key_steps, "q_send": [q_send], "home_q": [home_q]}
    i32 = jnp.int32
    tiles = shape(homes, 8, LANES, dtype=F32)
    home_o, home_logs = call(
        functools.partial(forward_kernel, heads, scale, parts),
        3,
        [block, tiles],
        [nbr, live, live_count, home_q, *stored],
        12 << 30,
    )
    marks["home_o"] = [home_o]
    logs_to = home_logs.reshape(n_dp, cap, 8, LANES)
    if OPT["lk"] == "shift":
        back_logs = jnp.concatenate(
            [shift(lax.dynamic_index_in_dim(logs_to, (mine + r) % n_dp, 0, keepdims=False), "dp", r) for r in range(n_dp)]
        )
    else:
        back_logs = trade(home_logs)
    marks["logs"] = [back_logs]
    back_o = trade(after(home_o, back_logs) if OPT["lf"] else home_o, OPT["ok"], -1)

    def gate(x, name):
        return after(x, *marks[OPT[name]]) if marks[OPT[name]] else x

    late_cot, late_proj = gate((cotangent, out_proj), "up0")
    cots = [late_cot]
    if gather_rows:
        cots = [jnp.where(enc == 0, late_cot, jnp.roll(late_cot, half, 0))]
        first = line_first_pick(*gate((c_ups[1], c_downs[1]), "x1"), mine)
        halves = [(first, swap(first, "enc", 1))]
        c_ups[3], c_downs[3] = line_last(*gate((c_ups[2], c_downs[2]), "c3"), "dp")
        c_ups[2], c_downs[2] = gate((c_ups[2], c_downs[2]), "x2")
        halves += [(x, swap(x, "enc", 1)) for x in line_pick(c_ups, c_downs, mine)[2:]]

    def proj_rows(k):
        return lax.dynamic_slice_in_dim(late_proj, (place ^ k) * hw, hw, 0)

    even_rows = jnp.concatenate([proj_rows(k) for k in bits[::2]], axis=0)
    odd_rows = jnp.concatenate([proj_rows(k) for k in bits[1::2]], axis=0)

    def upstream_of(cot):
        given = swap(dot(cot, odd_rows, ((1,), (1,))).astype(BF16), "fsdp", 1)
        pair = dot(cot, even_rows, ((1,), (1,))) + given.astype(F32)
        total = pair[:, :hw]
        for k in bits[2::2]:
            total += swap(pair[:, k // 2 * hw : (k // 2 + 1) * hw].astype(BF16), "fsdp", k).astype(F32)
        return total.astype(BF16).reshape(-1, SPAN, hw)

    ups = [upstream_of(cots[0])]
    if gather_rows and OPT["up1"] != "att":
        cots.append(jnp.concatenate(gate(halves[0], "up1"), axis=0))
        ups.append(upstream_of(cots[1]))
    if gather_rows and OPT["up1"] != "att" and OPT["up2"] != "att":
        cots.append(jnp.concatenate(gate(halves[1], "up2"), axis=0))
        ups.append(upstream_of(cots[2]))
    heads_of_bin = shape(spans, SPAN, hw)
    att_heads, att_turned, stats = call(
        functools.partial(join_kernel, heads, n_dp, OPT["lk"] == "shift"), 3, [heads_of_bin, heads_of_bin, tiles],
        [at, spot, on, back_logs, back_o, ups[0]], 5 << 30,
    )
    att_heads, att_turned = att_heads.reshape(bin_rows, hw), att_turned.reshape(bin_rows, hw)
    home_stats = trade(stats)
    if gather_rows:
        payload = att_turned
        if OPT["yh"]:
            payload = jnp.concatenate([att_turned, swap(att_turned[:, : hw // 2], "fsdp", 2)], axis=1)
        a_ups, a_downs = line_steps(payload, "dp")
        marks["att"], marks["stats"] = [att_turned], [home_stats]
        for k in range(len(cots), 3):
            cots.append(jnp.concatenate(after(halves[k - 1], att_turned), axis=0))
            ups.append(upstream_of(cots[k]))
        last_half = gate(halves[2], "up3")
        cots.append(jnp.concatenate(last_half, axis=0))
        ups += [upstream_of(x) for x in last_half] if OPT["half"] else [upstream_of(cots[3])]
        step_of = jnp.array([[order.index(b) for b in range(4)] for order in ORDER], i32)[mine]
        home_up = jnp.concatenate(ups, axis=0)
        up_at = step_of[bin_at] * spans + (span_at + turn) % spans
        hop = 2 if OPT["ag"] == "a2" else 1
        late_att, late_first = after((att_heads, payload), home_stats, a_ups[hop], a_downs[hop])
        if OPT["yg"]:
            late_att = after(late_att, home_up)
        if OPT["yg"] == 1:
            late_first = after(late_first, home_up)
        hop = 2 if OPT["bw"] == "a2" else 1
        home_stats = after(home_stats, a_ups[hop], a_downs[hop])
    else:
        home_up = trade(call(functools.partial(pick_kernel, spans), 2, block, [at, send, ups[0]], 1 << 30))
        up_at = jnp.arange(homes, dtype=i32)
        late_att = att_heads
    home_gq, grad_k, grad_v = call(
        functools.partial(backward_kernel, heads, scale, parts),
        5,
        [block] + [shape(n_f, group, piece_rows, hw)] * 2,
        [at, nbr, live, live_count, up_at, home_stats, home_q, home_up, *stored],
        30 << 30,
        [pltpu.VMEM((group, nbr_len, hw), F32)] * 2,
    )

    firsts = []
    att_evens, att_odds = exchange(late_att, 0, firsts)
    if gather_rows:
        att = line_pick(a_ups, a_downs, mine)
        bar = OPT["bar"]

        def cross(x):
            return swap(x[:, hw // 2 : hw] if OPT["yh"] else x, "fsdp", 2)

        crossed = [cross(x) for x in ([late_first] + att[1:])[:bar]]
        if OPT["frst"]:
            firsts = lax.optimization_barrier((firsts, home_gq))[0]
            home_gq, grad_k, grad_v = after((home_gq, grad_k, grad_v), *firsts)
        keep = min(bar + 1, 4)
        home_gq, grad_k, grad_v, att[:keep], crossed = lax.optimization_barrier(
            (home_gq, grad_k, grad_v, att[:keep], crossed)
        )
        if OPT["gg"] == "a3":
            home_gq = after(home_gq, a_ups[3], a_downs[3])
        if OPT["late"]:
            att[bar:] = after(att[bar:], home_gq)
        crossed += [cross(x) for x in att[bar:]]
        far = [jnp.concatenate([x[:, hw:], y], axis=1) for x, y in zip(att, crossed)] if OPT["yh"] else crossed
        near = [x[:, :hw] for x in att] if OPT["yh"] else att
        early_cot = jnp.concatenate(cots[:-1], axis=0)
        grad_proj = jnp.zeros((width, proj_cols), BF16)
        for k, blocks in ((0, near), (2, far)):
            early, last = jnp.concatenate(blocks[:-1], axis=0), blocks[-1]
            for bit, early_k, last_k in ((k, early, last), (k ^ 1, swap(early, "fsdp", 1), swap(last, "fsdp", 1))):
                if OPT["ld"]:
                    early_k = after(early_k, last_k)
                term = dot(early_k, early_cot, ((0,), (0,))) + dot(last_k, cots[-1], ((0,), (0,)))
                grad_proj = lax.dynamic_update_slice(grad_proj, term.astype(BF16), ((place ^ bit) * hw, jnp.int32(0)))
    else:
        gathered = lax.all_gather(att_heads, "fsdp", axis=1, tiled=True)
        grad_proj = lax.psum(dot(gathered, cotangent, ((0,), (0,))).astype(BF16), "dp")
    firsts = []
    grad_keys = to_rows(*exchange(grad_k, 0, firsts), (group, piece_rows))
    grad_values = to_rows(*exchange(after(grad_v, *firsts) if OPT["gv"] else grad_v, 0), (group, piece_rows))
    attended = to_rows(att_evens, att_odds, (token_rows,))
    gq_heads = call(sum_kernel, 2, heads_of_bin, [spot, on, trade(home_gq, OPT["gk"], -1)], 3 << 30).reshape(bin_rows, hw)
    grad_queries = to_rows(*exchange(gq_heads, 0), (token_rows,))
    return (attended, grad_queries, grad_keys, grad_values, grad_proj)


def solution(mesh):
    placed = (
        P(("dp", "fsdp"), "enc"),
        P("dp", "fsdp", "enc"),
        P("dp", "fsdp", "enc"),
        P("enc", "fsdp"),
        P(),
        P(),
        P(),
        P("dp", "fsdp"),
    )
    return jax.shard_map(
        local,
        mesh=mesh,
        in_specs=placed,
        out_specs=(
            P(("dp", "fsdp"), "enc"),
            P(("dp", "fsdp"), "enc"),
            P("dp", "fsdp", "enc"),
            P("dp", "fsdp", "enc"),
            P("enc", "fsdp"),
        ),
        check_vma=False,
    )
```

```python
import functools
import math

import jax
import jax.numpy as jnp
from jax import lax
from jax.experimental import pallas as pl
from jax.experimental.pallas import tpu as pltpu
from jax.sharding import PartitionSpec as P

HEAD_DIM = 128
SPAN = 64
SLOTS = 2
LANES = 128
LOW = -1e30
OPT = dict(
    yh=0, gg="", ld=0, late=0, qg=0, kg="q_send", c2="", c3="", x1="home_q", x2="", up0="key", up1="home_o",
    up2="att", up3="stats", half=1, lk="a2a", lf=0, ok="a2a", gk="a2a", ag="a1", bar=3, frst=0, gv=1, bw="a2", yg=2,
)
BF16 = jnp.bfloat16
F32 = jnp.float32


def dot(a, b, dims):
    return lax.dot_general(a, b, ((dims[0], dims[1]), ((), ())), preferred_element_type=F32)


def neighbour_head(refs, n, cols):
    evens, odds = refs[:-1], refs[-1]
    return jnp.concatenate([x for k, ref in enumerate(evens) for x in (ref[n, :, cols], odds[k, n, :, cols])], axis=0)


def columns_of(rows):
    return jnp.concatenate([rows, jnp.zeros((LANES - rows.shape[0], LANES), F32)], axis=0).T


def rows_of(columns):
    lane = lax.broadcasted_iota(jnp.int32, (SPAN, LANES), 1)
    table = jnp.zeros((SPAN, LANES), F32)
    for h, column in enumerate(columns):
        table = jnp.where(lane == h, column, table)
    return table.T[:8, :]


def index_kernel(n_dp, spans, cap, at_ref, src_ref, idx_ref, count_ref,
                 spot_ref, on_ref, nbr_ref, bin_ref, span_ref, send_ref, list_ref, size_ref, live_ref, seen_ref):
    mine = at_ref[0]
    slots = spans * SLOTS

    def clear(j, carry):
        for ref in (nbr_ref, live_ref, bin_ref, span_ref, send_ref, list_ref):
            ref[j] = 0
        return carry

    lax.fori_loop(0, n_dp * cap, clear, 0)

    def one_bin(b, carry):
        def reset(g, inner):
            seen_ref[g] = 0
            return inner

        lax.fori_loop(0, n_dp, reset, 0)

        def one_span(c, inner):
            count = count_ref[b * spans + c]
            for s in range(SLOTS):
                group = src_ref[b * spans + c, s]
                rank = seen_ref[group]
                seen_ref[group] = rank + 1
                on = (s < count).astype(jnp.int32)

                @pl.when(group == mine)
                def _(rank=rank, on=on, s=s):
                    j = b * cap + rank
                    nbr_ref[j] = idx_ref[b * spans + c, s]
                    live_ref[j] = on
                    bin_ref[j] = b
                    span_ref[j] = c

                @pl.when(b == mine)
                def _(group=group, rank=rank, on=on, s=s):
                    send_ref[group * cap + rank] = c
                    spot_ref[c * SLOTS + s] = group * cap + rank
                    on_ref[c * SLOTS + s] = on

            return inner

        lax.fori_loop(0, spans, one_span, 0)
        return carry

    lax.fori_loop(0, n_dp, one_bin, 0)

    def gather(j, size):
        @pl.when(live_ref[j] != 0)
        def _():
            list_ref[size] = j

        return size + live_ref[j]

    size = lax.fori_loop(0, n_dp * cap, gather, 0)
    size_ref[0] = size

    def fill(j, carry):
        @pl.when(jnp.logical_and(live_ref[j] == 0, size % 2 == 1))
        def _():
            list_ref[size] = j

        return carry

    lax.fori_loop(0, n_dp * cap, fill, 0)


def pick_kernel(per, at_ref, span_ref, *refs):
    parts, out_ref = refs[:-1], refs[-1]

    def one(j, carry):
        c = span_ref[j]
        if len(parts) == 1:
            out_ref[j] = parts[0][c]
        else:
            step = lax.div(c, per) ^ at_ref[1]
            for k, ref in enumerate(parts[:-1]):

                @pl.when(step == 2 * k)
                def _(ref=ref):
                    out_ref[j] = ref[lax.rem(c, per)]

            @pl.when(step % 2 == 1)
            def _():
                out_ref[j] = parts[-1][step // 2, lax.rem(c, per)]

        return carry

    lax.fori_loop(0, out_ref.shape[0], one, 0)


def forward_kernel(heads, scale, parts, nbr_ref, live_ref, size_ref, q_ref, *refs):
    k_refs, v_refs = refs[:parts], refs[parts : 2 * parts]
    o_ref, out_ref = refs[2 * parts :]

    def pair(i, carry):
        logs = [[], []]
        for h in range(heads):
            cols = slice(h * HEAD_DIM, (h + 1) * HEAD_DIM)
            for u in range(2):
                r = live_ref[2 * i + u]
                n = nbr_ref[r]
                scores = dot(q_ref[r, :, cols], neighbour_head(k_refs, n, cols), ((1,), (1,))) * scale
                peak = jnp.max(scores, axis=1, keepdims=True)
                expo = jnp.exp(scores - peak)
                total = jnp.sum(expo, axis=1, keepdims=True)
                part = dot(expo.astype(BF16), neighbour_head(v_refs, n, cols), ((1,), (0,)))
                o_ref[r, :, cols] = (part / total).astype(BF16)
                logs[u].append(peak + jnp.log(total))
        for u in range(2):
            out_ref[live_ref[2 * i + u]] = jnp.concatenate([rows_of(logs[u]), jnp.zeros((8, LANES - SPAN), F32)], axis=1)
        return carry

    lax.fori_loop(0, (size_ref[0] + 1) // 2, pair, 0)


def join_kernel(heads, n_dp, shifted, at_ref, spot_ref, on_ref, stats_ref, block_ref, up_ref, out_ref, turned_ref, send_ref):
    spans = out_ref.shape[0]
    cap = send_ref.shape[0] // n_dp
    send_ref[...] = jnp.zeros_like(send_ref)

    def span(c, carry):
        turned = lax.rem(c + at_ref[2], spans)
        spots = [spot_ref[c * SLOTS + s] for s in range(SLOTS)]
        on = [on_ref[c * SLOTS + s] != 0 for s in range(SLOTS)]
        came = spots
        if shifted:
            came = [lax.rem(at_ref[0] - lax.div(x, cap) + n_dp, n_dp) * cap + lax.rem(x, cap) for x in spots]
        logs = [jnp.where(o, stats_ref[x][:, :SPAN], LOW) for o, x in zip(on, came)]
        peak = functools.reduce(jnp.maximum, logs)
        expos = [jnp.exp(x - peak) for x in logs]
        total = sum(expos)
        columns = columns_of(jnp.concatenate([x / total for x in expos], axis=1))
        centres = []
        for h in range(heads):
            cols = slice(h * HEAD_DIM, (h + 1) * HEAD_DIM)
            joined = jnp.zeros((SPAN, HEAD_DIM), F32)
            for s in range(SLOTS):
                part = block_ref[spots[s], :, cols].astype(F32) * columns[s * SPAN : (s + 1) * SPAN, h : h + 1]
                joined += jnp.where(on[s], part, 0.0)
            out_ref[c, :, cols] = joined.astype(BF16)
            turned_ref[turned, :, cols] = joined.astype(BF16)
            centres.append(jnp.sum(joined * up_ref[turned, :, cols].astype(F32), axis=1, keepdims=True))
        tile = jnp.concatenate([peak + jnp.log(total), rows_of(centres)], axis=1)
        for s in range(SLOTS):
            send_ref[spots[s]] = tile
        return carry

    lax.fori_loop(0, spans, span, 0)


def backward_kernel(heads, scale, parts, at_ref, nbr_ref, live_ref, size_ref, upat_ref, stats_ref, q_ref, up_ref, *refs):
    k_refs, v_refs = refs[:parts], refs[parts : 2 * parts]
    gq_ref, gk_ref, gv_ref, acc_k, acc_v = refs[2 * parts :]
    n_f, _, piece_rows, _ = gk_ref.shape

    acc_k[...] = jnp.zeros_like(acc_k)
    acc_v[...] = jnp.zeros_like(acc_v)

    def pair(i, carry):
        at = [live_ref[2 * i + u] for u in range(2)]
        valid = [2 * i + u < size_ref[0] for u in range(2)]
        columns = [columns_of(stats_ref[r]) for r in at]
        for h in range(heads):
            cols = slice(h * HEAD_DIM, (h + 1) * HEAD_DIM)
            found = []
            for u, r in enumerate(at):
                n = nbr_ref[r]
                q, up = q_ref[r, :, cols], up_ref[upat_ref[r], :, cols]
                keys, values = neighbour_head(k_refs, n, cols), neighbour_head(v_refs, n, cols)
                scores = dot(q, keys, ((1,), (1,))) * scale
                dprobs = dot(up, values, ((1,), (1,)))
                probs = jnp.exp(scores - columns[u][:SPAN, h : h + 1])
                dscores = probs * (dprobs - columns[u][SPAN:, h : h + 1]) * scale
                probs_b = jnp.where(valid[u], probs, 0.0).astype(BF16)
                dscores = jnp.where(valid[u], dscores, 0.0).astype(BF16)
                gq_ref[r, :, cols] = dot(dscores, keys, ((1,), (0,))).astype(BF16)
                found.append((n, dot(dscores, q, ((0,), (0,))), dot(probs_b, up, ((0,), (0,)))))
            for n, key_part, value_part in found:
                acc_k[n, :, cols] += key_part
                acc_v[n, :, cols] += value_part
        return carry

    lax.fori_loop(0, (size_ref[0] + 1) // 2, pair, 0)

    def neighbour(n, carry):
        for p in range(n_f):
            rows = slice(p * piece_rows, (p + 1) * piece_rows)
            gk_ref[at_ref[1] ^ p, n] = acc_k[n, rows, :].astype(BF16)
            gv_ref[at_ref[1] ^ p, n] = acc_v[n, rows, :].astype(BF16)
        return carry

    lax.fori_loop(0, acc_k.shape[0], neighbour, 0)


def sum_kernel(spot_ref, on_ref, block_ref, out_ref):
    def span(c, carry):
        total = jnp.zeros(out_ref.shape[1:], F32)
        for s in range(SLOTS):
            at = c * SLOTS + s
            total += jnp.where(on_ref[at] != 0, block_ref[spot_ref[at]].astype(F32), 0.0)
        out_ref[c] = total.astype(BF16)
        return carry

    lax.fori_loop(0, out_ref.shape[0], span, 0)


def line_steps(x, axis, gates={}):
    ups, downs = [x], [x]
    for k in range(1, lax.axis_size(axis)):
        up, down = after((ups[-1], downs[-1]), *gates[k]) if k in gates else (ups[-1], downs[-1])
        up, down = line_last(up, down, axis)
        ups.append(up)
        downs.append(down)
    return ups, downs


def line_last(up, down, axis):
    n = lax.axis_size(axis)
    rise = [(i, i + 1) for i in range(n - 1)]
    fall = [(i + 1, i) for i in range(n - 1)]
    return lax.ppermute(up, axis, rise), lax.ppermute(down, axis, fall)


ORDER = ((0, 1, 2, 3), (1, 0, 2, 3), (2, 1, 3, 0), (3, 2, 1, 0))


def line_first_pick(up, down, mine):
    return jnp.where(mine == 0, down, up)


def line_pick(ups, downs, mine):
    first = line_first_pick(ups[1], downs[1], mine)
    ups2, downs2 = after((ups[2], downs[2]), first)
    second = jnp.where(mine == 0, downs2, jnp.where(mine == 3, ups2, downs[1]))
    inner = jnp.where(mine == 1, downs2, ups2)
    ups3, downs3 = after((ups[3], downs[3]), second)
    third = jnp.where(mine == 0, downs3, jnp.where(mine == 3, ups3, inner))
    return [ups[0], first, second, third]


def swap(x, axis, bits):
    return lax.ppermute(x, axis, [(i, i ^ bits) for i in range(lax.axis_size(axis))])


def shift(x, axis, by):
    n = lax.axis_size(axis)
    if by % n == 0:
        return x
    return lax.ppermute(x, axis, [(i, (i + by) % n) for i in range(n)])


def after(x, *others):
    return lax.optimization_barrier((x, *others))[0]


def local(queries, nbr_keys, nbr_values, out_proj, nbr_source, nbr_index, nbr_count, cotangent):
    n_dp, n_f, n_e = lax.axis_size("dp"), lax.axis_size("fsdp"), lax.axis_size("enc")
    token_rows, width = queries.shape
    hw = width // n_f
    heads = hw // HEAD_DIM
    spans_here = token_rows // SPAN
    spans = spans_here * n_f
    slots = spans * SLOTS
    cap = (spans_here * SLOTS + n_dp - 1) // n_dp * n_f
    group, piece_rows, _ = nbr_keys.shape
    nbr_len = piece_rows * n_f
    bin_rows = token_rows * n_f
    homes = n_dp * cap
    proj_cols = cotangent.shape[1]
    scale = 1.0 / math.sqrt(HEAD_DIM)
    mine = lax.axis_index("dp")
    place = lax.axis_index("fsdp")
    enc = lax.axis_index("enc")
    core = place % 2
    chip = place - core
    bits = range(n_f)
    half = bin_rows // 2
    raw = (n_dp - 1) * bin_rows * (hw + proj_cols // n_e)
    summed = 2 * width * proj_cols * (n_dp - 1) // n_dp
    gather_rows = raw <= summed and (n_e, n_dp, n_f) == (2, 4, 4) and half % SPAN == 0
    turn = enc * (spans // 2) if gather_rows else jnp.int32(0)
    at = jnp.stack([mine, place, turn]).astype(jnp.int32)

    full = pl.BlockSpec(memory_space=pltpu.VMEM)
    smem = pl.BlockSpec(memory_space=pltpu.SMEM)

    def call(kernel, n_smem, outs, args, flops, scratch=()):
        single = not isinstance(outs, list)
        shapes = [outs] if single else outs
        specs = [smem if len(o.shape) == 1 else full for o in shapes]
        return pl.pallas_call(
            kernel,
            in_specs=[smem] * n_smem + [full] * (len(args) - n_smem),
            out_specs=specs[0] if single else specs,
            out_shape=outs,
            scratch_shapes=scratch,
            compiler_params=pltpu.CompilerParams(vmem_limit_bytes=56 << 20),
            cost_estimate=pl.CostEstimate(flops=flops, bytes_accessed=0, transcendentals=0),
        )(*args)

    def shape(*dims, dtype=BF16):
        return jax.ShapeDtypeStruct(dims, dtype)

    def exchange(x, dim, firsts=None, gates=()):
        size = x.shape[dim] // n_f

        def cut(y, start, count=1):
            return lax.dynamic_slice_in_dim(y, start * size, count * size, dim)

        got = [swap(cut(x, chip ^ k, 2), "fsdp", k) for k in bits[2::2]]
        if firsts is not None:
            firsts.extend(got)
        if gates:
            x, got = after((x, got), *gates)
        odds = swap(jnp.stack([cut(x, place ^ 1)] + [cut(y, 1 - core) for y in got]), "fsdp", 1)
        return [cut(x, place)] + [cut(y, core) for y in got], odds

    def to_rows(evens, odds, rows):
        out = jnp.zeros(rows + (width,), BF16)
        for k in bits:
            start = (jnp.int32(0),) * len(rows) + ((place ^ k) * hw,)
            x = odds[k // 2] if k % 2 else evens[k // 2]
            out = lax.dynamic_update_slice(out, x.reshape(rows + (hw,)), start)
        return out

    def trade(x, kind="a2a", sign=1):
        if kind == "a2a":
            return lax.all_to_all(x, "dp", split_axis=0, concat_axis=0, tiled=True)
        to = x.reshape((n_dp, -1) + x.shape[1:])
        got = [shift(lax.dynamic_index_in_dim(to, (mine + r) % n_dp, 0, keepdims=False), "dp", r) for r in range(n_dp)]
        out = jnp.zeros_like(to)
        for r, y in enumerate(got):
            out = lax.dynamic_update_index_in_dim(out, y, (mine - r) % n_dp, 0)
        return out.reshape(x.shape)

    i32 = jnp.int32
    spot, on, nbr, bin_at, span_at, send, live, live_count = call(
        functools.partial(index_kernel, n_dp, spans, cap),
        4,
        [shape(slots, dtype=i32)] * 2 + [shape(homes, dtype=i32)] * 5 + [shape(1, dtype=i32)],
        [at, nbr_source, nbr_index, nbr_count],
        1 << 30,
        [pltpu.SMEM((homes,), i32), pltpu.SMEM((n_dp,), i32)],
    )

    q_evens, q_odds = exchange(queries, 1, None, [send] if OPT["qg"] else ())
    block = shape(homes, SPAN, hw)
    q_parts = [x.reshape(spans_here, SPAN, hw) for x in q_evens] + [q_odds.reshape(n_f // 2, spans_here, SPAN, hw)]
    q_send = call(functools.partial(pick_kernel, spans_here), 2, block, [at, send] + q_parts, 1 << 30)
    home_q = trade(q_send)

    if gather_rows:
        own_half = lax.dynamic_slice_in_dim(cotangent, enc * half, half, 0)
        c_ups, c_downs = line_steps(own_half, "dp", {2: [home_q]} if OPT["c2"] else {})


    key_steps = []
    k_evens, k_odds = exchange(after(nbr_keys, q_send if OPT["kg"] == "q_send" else q_odds), 2, key_steps)
    line_first = [c_ups[1], c_downs[1]] if gather_rows else []
    v_evens, v_odds = exchange(after(nbr_values, *key_steps, *line_first), 2)
    stored = [*k_evens, k_odds, *v_evens, v_odds]
    parts = n_f // 2 + 1

    marks = {"": [], "key": key_steps, "q_send": [q_send], "home_q": [home_q]}
    i32 = jnp.int32
    tiles = shape(homes, 8, LANES, dtype=F32)
    home_o, home_logs = call(
        functools.partial(forward_kernel, heads, scale, parts),
        3,
        [block, tiles],
        [nbr, live, live_count, home_q, *stored],
        12 << 30,
    )
    marks["home_o"] = [home_o]
    logs_to = home_logs.reshape(n_dp, cap, 8, LANES)
    if OPT["lk"] == "shift":
        back_logs = jnp.concatenate(
            [shift(lax.dynamic_index_in_dim(logs_to, (mine + r) % n_dp, 0, keepdims=False), "dp", r) for r in range(n_dp)]
        )
    else:
        back_logs = trade(home_logs)
    marks["logs"] = [back_logs]
    back_o = trade(after(home_o, back_logs) if OPT["lf"] else home_o, OPT["ok"], -1)

    def gate(x, name):
        return after(x, *marks[OPT[name]]) if marks[OPT[name]] else x

    late_cot, late_proj = gate((cotangent, out_proj), "up0")
    cots = [late_cot]
    if gather_rows:
        cots = [jnp.where(enc == 0, late_cot, jnp.roll(late_cot, half, 0))]
        first = line_first_pick(*gate((c_ups[1], c_downs[1]), "x1"), mine)
        halves = [(first, swap(first, "enc", 1))]
        c_ups[3], c_downs[3] = line_last(*gate((c_ups[2], c_downs[2]), "c3"), "dp")
        c_ups[2], c_downs[2] = gate((c_ups[2], c_downs[2]), "x2")
        halves += [(x, swap(x, "enc", 1)) for x in line_pick(c_ups, c_downs, mine)[2:]]

    def proj_rows(k):
        return lax.dynamic_slice_in_dim(late_proj, (place ^ k) * hw, hw, 0)

    even_rows = jnp.concatenate([proj_rows(k) for k in bits[::2]], axis=0)
    odd_rows = jnp.concatenate([proj_rows(k) for k in bits[1::2]], axis=0)

    def upstream_of(cot):
        given = swap(dot(cot, odd_rows, ((1,), (1,))).astype(BF16), "fsdp", 1)
        pair = dot(cot, even_rows, ((1,), (1,))) + given.astype(F32)
        total = pair[:, :hw]
        for k in bits[2::2]:
            total += swap(pair[:, k // 2 * hw : (k // 2 + 1) * hw].astype(BF16), "fsdp", k).astype(F32)
        return total.astype(BF16).reshape(-1, SPAN, hw)

    ups = [upstream_of(cots[0])]
    if gather_rows and OPT["up1"] != "att":
        cots.append(jnp.concatenate(gate(halves[0], "up1"), axis=0))
        ups.append(upstream_of(cots[1]))
    if gather_rows and OPT["up1"] != "att" and OPT["up2"] != "att":
        cots.append(jnp.concatenate(gate(halves[1], "up2"), axis=0))
        ups.append(upstream_of(cots[2]))
    heads_of_bin = shape(spans, SPAN, hw)
    att_heads, att_turned, stats = call(
        functools.partial(join_kernel, heads, n_dp, OPT["lk"] == "shift"), 3, [heads_of_bin, heads_of_bin, tiles],
        [at, spot, on, back_logs, back_o, ups[0]], 5 << 30,
    )
    att_heads, att_turned = att_heads.reshape(bin_rows, hw), att_turned.reshape(bin_rows, hw)
    home_stats = trade(stats)
    if gather_rows:
        payload = att_turned
        if OPT["yh"]:
            payload = jnp.concatenate([att_turned, swap(att_turned[:, : hw // 2], "fsdp", 2)], axis=1)
        a_ups, a_downs = line_steps(payload, "dp")
        marks["att"], marks["stats"] = [att_turned], [home_stats]
        for k in range(len(cots), 3):
            cots.append(jnp.concatenate(after(halves[k - 1], att_turned), axis=0))
            ups.append(upstream_of(cots[k]))
        last_half = gate(halves[2], "up3")
        cots.append(jnp.concatenate(last_half, axis=0))
        ups += [upstream_of(x) for x in last_half] if OPT["half"] else [upstream_of(cots[3])]
        step_of = jnp.array([[order.index(b) for b in range(4)] for order in ORDER], i32)[mine]
        home_up = jnp.concatenate(ups, axis=0)
        up_at = step_of[bin_at] * spans + (span_at + turn) % spans
        hop = 2 if OPT["ag"] == "a2" else 1
        late_att, late_first = after((att_heads, payload), home_stats, a_ups[hop], a_downs[hop])
        if OPT["yg"]:
            late_att = after(late_att, home_up)
        if OPT["yg"] == 1:
            late_first = after(late_first, home_up)
        hop = 2 if OPT["bw"] == "a2" else 1
        home_stats = after(home_stats, a_ups[hop], a_downs[hop])
    else:
        home_up = trade(call(functools.partial(pick_kernel, spans), 2, block, [at, send, ups[0]], 1 << 30))
        up_at = jnp.arange(homes, dtype=i32)
        late_att = att_heads
    home_gq, grad_k, grad_v = call(
        functools.partial(backward_kernel, heads, scale, parts),
        5,
        [block] + [shape(n_f, group, piece_rows, hw)] * 2,
        [at, nbr, live, live_count, up_at, home_stats, home_q, home_up, *stored],
        30 << 30,
        [pltpu.VMEM((group, nbr_len, hw), F32)] * 2,
    )

    firsts = []
    att_evens, att_odds = exchange(late_att, 0, firsts)
    if gather_rows:
        att = line_pick(a_ups, a_downs, mine)
        bar = OPT["bar"]

        def cross(x):
            return swap(x[:, hw // 2 : hw] if OPT["yh"] else x, "fsdp", 2)

        crossed = [cross(x) for x in ([late_first] + att[1:])[:bar]]
        if OPT["frst"]:
            firsts = lax.optimization_barrier((firsts, home_gq))[0]
            home_gq, grad_k, grad_v = after((home_gq, grad_k, grad_v), *firsts)
        keep = min(bar + 1, 4)
        home_gq, grad_k, grad_v, att[:keep], crossed = lax.optimization_barrier(
            (home_gq, grad_k, grad_v, att[:keep], crossed)
        )
        if OPT["gg"] == "a3":
            home_gq = after(home_gq, a_ups[3], a_downs[3])
        if OPT["late"]:
            att[bar:] = after(att[bar:], home_gq)
        crossed += [cross(x) for x in att[bar:]]
        far = [jnp.concatenate([x[:, hw:], y], axis=1) for x, y in zip(att, crossed)] if OPT["yh"] else crossed
        near = [x[:, :hw] for x in att] if OPT["yh"] else att
        early_cot = jnp.concatenate(cots[:-1], axis=0)
        grad_proj = jnp.zeros((width, proj_cols), BF16)
        for k, blocks in ((0, near), (2, far)):
            early, last = jnp.concatenate(blocks[:-1], axis=0), blocks[-1]
            for bit, early_k, last_k in ((k, early, last), (k ^ 1, swap(early, "fsdp", 1), swap(last, "fsdp", 1))):
                if OPT["ld"]:
                    early_k = after(early_k, last_k)
                term = dot(early_k, early_cot, ((0,), (0,))) + dot(last_k, cots[-1], ((0,), (0,)))
                grad_proj = lax.dynamic_update_slice(grad_proj, term.astype(BF16), ((place ^ bit) * hw, jnp.int32(0)))
    else:
        gathered = lax.all_gather(att_heads, "fsdp", axis=1, tiled=True)
        grad_proj = lax.psum(dot(gathered, cotangent, ((0,), (0,))).astype(BF16), "dp")
    firsts = []
    grad_keys = to_rows(*exchange(grad_k, 0, firsts), (group, piece_rows))
    grad_values = to_rows(*exchange(after(grad_v, *firsts) if OPT["gv"] else grad_v, 0), (group, piece_rows))
    attended = to_rows(att_evens, att_odds, (token_rows,))
    gq_heads = call(sum_kernel, 2, heads_of_bin, [spot, on, trade(home_gq, OPT["gk"], -1)], 3 << 30).reshape(bin_rows, hw)
    grad_queries = to_rows(*exchange(gq_heads, 0), (token_rows,))
    return (attended, grad_queries, grad_keys, grad_values, grad_proj)


def solution(mesh):
    placed = (
        P(("dp", "fsdp"), "enc"),
        P("dp", "fsdp", "enc"),
        P("dp", "fsdp", "enc"),
        P("enc", "fsdp"),
        P(),
        P(),
        P(),
        P("dp", "fsdp"),
    )
    return jax.shard_map(
        local,
        mesh=mesh,
        in_specs=placed,
        out_specs=(
            P(("dp", "fsdp"), "enc"),
            P(("dp", "fsdp"), "enc"),
            P("dp", "fsdp", "enc"),
            P("dp", "fsdp", "enc"),
            P("enc", "fsdp"),
        ),
        check_vma=False,
    )
```
